32 devices in a mesh: section: 4 (over z), seq: 8 (over y, x, core).
Axes of the slice: x: 2, y: 2, z: 4, core: 2. Of those that a mesh axis runs over, the one named last changes fastest.
Arguments:
- section_input: bfloat16 [4, 8192, 1024], P('section', 'seq'), may hold values from -6 to 6
- stashed_input: bfloat16 [4, 8192, 1024], P('section', 'seq'), may hold values from -6 to 6
- output_grad: bfloat16 [4, 8192, 1024], P('section', 'seq'), may hold values from -6 to 6
- gain_mixer: float32 [4, 1024], P('section'), may hold values from 0.1 to 1.9
- gain_channel: float32 [4, 1024], P('section'), may hold values from 0.1 to 1.9
- factor_first: bfloat16 [4, 64, 128, 128], P('section', 'seq'), may hold values from -0.5 to 0.5
- factor_second: bfloat16 [4, 128, 64, 64], P('section', 'seq'), may hold values from -0.75 to 0.75
- spectrum: bfloat16 [4, 64, 128, 1024], P('section', None, 'seq'), may hold values from -6 to 6
- factor_third: bfloat16 [4, 128, 64, 64], P('section', 'seq'), may hold values from -0.75 to 0.75
- factor_fourth: bfloat16 [4, 64, 128, 128], P('section', 'seq'), may hold values from -0.5 to 0.5
- mixer_gate: bfloat16 [4, 1024, 256], P('section'), may hold values from -0.375 to 0.375
- channel_up: bfloat16 [4, 1024, 512], P('section'), may hold values from -0.375 to 0.375
- channel_gate: bfloat16 [4, 1024, 512], P('section'), may hold values from -0.375 to 0.375
- channel_down: bfloat16 [4, 2048, 256], P('section'), may hold values from -0.25 to 0.25
Outputs:
- next_input: bfloat16 [4, 8192, 1024], P('section', 'seq')
- upstream_grad: bfloat16 [4, 8192, 1024], P('section', 'seq')
- spectrum_grad: bfloat16 [4, 64, 128, 1024], P('section', None, 'seq')
- mixer_gate_grad: bfloat16 [4, 1024, 256], P('section', 'seq')
- channel_up_grad: bfloat16 [4, 1024, 512], P('section', 'seq')
- channel_gate_grad: bfloat16 [4, 1024, 512], P('section', 'seq')
- channel_down_grad: bfloat16 [4, 2048, 256], P('section', 'seq')
The draws below stay inside these ranges and needn't reach their ends.
All inputs are finite; a program needn't handle non-finite values.
Results may differ from the reference program's by a relative error of at most 0.017.
Values may be sent and summed in bfloat16 or wider, within the bound.
A program may use at most 128 MiB of HBM per device.

```python
import math
import jax
import jax.numpy as jnp
from jax import lax

D = 1024
FF = 2048
NB = 4
NI = 64
NJ = 128
L = 8192
SECTIONS = 4
N_SECTION = 4


def strengthened(values, stream_key, source, target, blocks, factor):
    def block_of(axis_at):
        return (jnp.arange(values.shape[axis_at]) // (values.shape[axis_at] // blocks)).reshape((-1,) + (1,) * (values.ndim - 1 - axis_at))

    one_side = jax.random.permutation(stream_key, blocks)[block_of(target)]
    second = (block_of(target) + blocks // 2) % blocks
    return jnp.where((block_of(source) == one_side) | (block_of(source) == second), factor * values, values)


def level_of(key, shape, pieces, smallest, top_value):
    def one(dim, shards_of):
        heights = jax.random.uniform(jax.random.fold_in(jax.random.fold_in(key, 6), dim), (shards_of,), jnp.float32, smallest / len(pieces), top_value / len(pieces))
        return jnp.repeat(jnp.exp(heights), shape[dim] // shards_of).reshape((-1,) + (1,) * (len(shape) - dim - 1))

    loudness = one(*pieces[0])
    for cut in pieces[1:]:
        loudness = loudness * one(*cut)
    return loudness


def gaussian(key, shape, scale, limit, shards=(), dtype=jnp.bfloat16):
    values = jax.random.normal(key, shape, jnp.float32) * scale
    if len(shards) > 0:
        values = level_of(key, shape, shards, -0.22, 0.18) * values
    return jnp.clip(values, min=-limit, max=limit).astype(dtype)


def gaussian_with(own_key, extent, deviation, bound, shards, heavy, kind=jnp.bfloat16):
    array = deviation * jax.random.normal(own_key, extent, jnp.float32)
    if shards:
        array = array * level_of(own_key, extent, shards, -0.22, 0.18)
    return jnp.clip(strengthened(array, jax.random.fold_in(own_key, 3), *heavy), -bound, bound).astype(kind)


def setup_inputs(seed: int = 0) -> dict:
    streams_of = jax.random.split(jax.random.key(seed), 15)
    return {
        "section_input": gaussian(streams_of[0], (SECTIONS, L, D), 1.0, 6.0, ((0, 4), (1, 8))),
        "stashed_input": gaussian_with(streams_of[1], (SECTIONS, L, D), 1.0, 6.0, ((0, 4), (1, 8)), (1, 2, 8, 2.0)),
        "output_grad": gaussian(streams_of[2], (SECTIONS, L, D), 1.0, 6.0, ((0, 4), (1, 8))),
        "gain_mixer": jnp.clip(1.0 + 0.18 * jax.random.normal(streams_of[3], (SECTIONS, D), jnp.float32), 0.1, 1.9),
        "gain_channel": jnp.clip(1.0 + 0.18 * jax.random.normal(streams_of[4], (SECTIONS, D), jnp.float32), 0.1, 1.9),
        "factor_first": gaussian(streams_of[5], (SECTIONS, NI, NJ, NJ), NJ ** -0.5, 0.5, ((0, 4), (1, 8))),
        "factor_second": gaussian(streams_of[6], (SECTIONS, NJ, NI, NI), NI ** -0.5, 0.75, ((0, 4), (1, 8))),
        "spectrum": gaussian(streams_of[7], (SECTIONS, NI, NJ, D), 1.0, 6.0, ((0, 4), (2, 8))),
        "factor_third": gaussian(streams_of[8], (SECTIONS, NJ, NI, NI), NI ** -0.5, 0.75, ((0, 4), (1, 8))),
        "factor_fourth": gaussian(streams_of[9], (SECTIONS, NI, NJ, NJ), NJ ** -0.5, 0.5, ((0, 4), (1, 8))),
        "mixer_gate": gaussian(streams_of[10], (SECTIONS, D, D // NB), (D // NB) ** -0.5, 0.375, ((0, 4),)),
        "channel_up": gaussian(streams_of[11], (SECTIONS, D, FF // NB), (D // NB) ** -0.5, 0.375, ((0, 4),)),
        "channel_gate": gaussian(streams_of[12], (SECTIONS, D, FF // NB), (D // NB) ** -0.5, 0.375, ((0, 4),)),
        "channel_down": gaussian(streams_of[13], (SECTIONS, FF, D // NB), (FF // NB) ** -0.5, 0.25, ((0, 4),)),
    }


epsilon = 1e-06

def bround(value):
    return lax.optimization_barrier(value.astype(jnp.bfloat16))

def widened_view(value):
    return value.astype(jnp.float32)

def rms_scale(value_array):
    return lax.rsqrt(lax.optimization_barrier(jnp.mean(value_array * value_array, axis=-1, keepdims=True)) + epsilon)

def norm_back(value_array, scale, gain, incoming_gradient):
    scaled = gain * incoming_gradient
    return scale * scaled - value_array * (scale * scale * scale) * lax.optimization_barrier(jnp.mean(scaled * value_array, axis=-1, keepdims=True))

def block_apply(value_array, weight, block_list):
    item_count = value_array.shape[0]
    reshaped_array = widened_view(weight).reshape(block_list, weight.shape[0] // block_list, weight.shape[1])
    final_output = jnp.einsum('ynq,nqd->ynd', widened_view(value_array).reshape(item_count, block_list, -1), reshaped_array)
    return final_output.reshape(item_count, -1)

def block_back(incoming_gradient, weight, block_list):
    item_count = incoming_gradient.shape[0]
    reshaped_array = widened_view(weight).reshape(block_list, weight.shape[0] // block_list, weight.shape[1])
    final_output = jnp.einsum('eaq,awq->eaw', widened_view(incoming_gradient).reshape(item_count, block_list, -1), reshaped_array)
    return final_output.reshape(item_count, -1)

def block_grad(value_array, incoming_gradient, block_list):
    item_count = value_array.shape[0]
    final_output = jnp.einsum('wli,wld->lid', widened_view(value_array).reshape(item_count, block_list, -1), widened_view(incoming_gradient).reshape(item_count, block_list, -1))
    return final_output.reshape(-1, final_output.shape[2])

def shuffle(value_array, block_list):
    item_count = value_array.shape[0]
    return value_array.reshape(item_count, block_list, block_list, -1).transpose(0, 2, 1, 3).reshape(item_count, -1)

def layer_forward(inputs, gain_one, second_gain, first, second, kernel_here, third, fourth_factor, mixing_weight, up_weight, activation_weight, down_weight):
    wide = widened_view(inputs)
    scale_one = rms_scale(wide)
    normed = bround(wide * scale_one * gain_one)
    folded = bround(jnp.einsum('iqj,ijc->iqc', widened_view(first), widened_view(normed).reshape(NI, NJ, -1)))
    mixed = jnp.einsum('jpi,ijc->pjc', widened_view(second), widened_view(folded))
    filtered = bround(mixed * widened_view(kernel_here))
    returned = bround(jnp.einsum('jpi,ijc->pjc', widened_view(third), widened_view(filtered)))
    back_mixed = jnp.einsum('iqj,ijc->iqc', widened_view(fourth_factor), widened_view(returned)).reshape(NI * NJ, -1)
    gating = block_apply(normed, mixing_weight, NB)
    middle = bround(wide + back_mixed * gating)
    middle_wide = widened_view(middle)
    scale_two = rms_scale(middle_wide)
    normed_two = bround(middle_wide * scale_two * second_gain)
    lifted = block_apply(normed_two, up_weight, NB)
    gated = block_apply(normed_two, activation_weight, NB)
    hidden = bround(jax.nn.silu(gated) * lifted)
    shuffled = shuffle(hidden, NB)
    output = bround(middle_wide + block_apply(shuffled, down_weight, NB))
    saved = (wide, scale_one, normed, mixed, back_mixed, gating, middle_wide, scale_two, normed_two, lifted, gated, shuffled)
    return (output, saved)

def layer_backward(saved, incoming_gradient, gain_one, second_gain, first, second, kernel_here, third, fourth_factor, mixing_weight, up_weight, activation_weight, down_weight):
    wide, scale_one, normed, mixed, back_mixed, gating, middle_wide, scale_two, normed_two, lifted, gated, shuffled = saved
    grad_factor = 1.0 / math.sqrt(NI * NJ)
    up_wide = widened_view(incoming_gradient)
    d_shuffled = bround(block_back(incoming_gradient, down_weight, NB))
    d_hidden = widened_view(shuffle(d_shuffled, NB))
    sigma = jax.nn.sigmoid(gated)
    d_lift = bround(d_hidden * gated * sigma)
    d_gated = bround(d_hidden * lifted * sigma * (1.0 + gated * (1.0 - sigma)))
    d_norm_two = block_back(d_lift, up_weight, NB) + block_back(d_gated, activation_weight, NB)
    d_middle = bround(up_wide + norm_back(middle_wide, scale_two, second_gain, d_norm_two))
    d_mid_wide = widened_view(d_middle)
    d_back = bround(d_mid_wide * gating)
    d_gating = bround(d_mid_wide * back_mixed)
    d_returned = bround(jnp.einsum('iqj,iqc->ijc', widened_view(fourth_factor), widened_view(d_back).reshape(NI, NJ, -1)))
    d_filtered = jnp.einsum('jpi,pjc->ijc', widened_view(third), widened_view(d_returned))
    kernel_grad = (d_filtered * mixed).astype(jnp.bfloat16)
    d_mixed = bround(d_filtered * widened_view(kernel_here))
    d_folded = bround(jnp.einsum('jpi,pjc->ijc', widened_view(second), widened_view(d_mixed)))
    d_normed = jnp.einsum('iqj,iqc->ijc', widened_view(first), widened_view(d_folded)).reshape(NI * NJ, -1)
    d_normed = d_normed + block_back(d_gating, mixing_weight, NB)
    d_input = (d_mid_wide + norm_back(wide, scale_one, gain_one, d_normed)).astype(jnp.bfloat16)
    mix_grad = (block_grad(normed, d_gating, NB) * grad_factor).astype(jnp.bfloat16)
    up_grad = (block_grad(normed_two, d_lift, NB) * grad_factor).astype(jnp.bfloat16)
    act_grad = (block_grad(normed_two, d_gated, NB) * grad_factor).astype(jnp.bfloat16)
    down_grad = (block_grad(shuffled, incoming_gradient, NB) * grad_factor).astype(jnp.bfloat16)
    return (d_input, kernel_grad, mix_grad, up_grad, act_grad, down_grad)

def reference(section_input, stashed_input, output_grad, gain_mixer, gain_channel, factor_first, factor_second, spectrum, factor_third, factor_fourth, mixer_gate, channel_up, channel_gate, channel_down):
    forward_outs = []
    input_grads = []
    kernel_grads = []
    mix_grads = []
    up_grads = []
    act_grads = []
    down_grads = []
    for section in range(N_SECTION):
        weights = (gain_mixer[section], gain_channel[section], factor_first[section], factor_second[section], spectrum[section], factor_third[section], factor_fourth[section], mixer_gate[section], channel_up[section], channel_gate[section], channel_down[section])
        output, unused = layer_forward(section_input[section], *weights)
        forward_outs.append(output)
        recomputed, saved = layer_forward(stashed_input[section], *weights)
        grads = layer_backward(saved, output_grad[section], *weights)
        input_grads.append(grads[0])
        kernel_grads.append(grads[1])
        mix_grads.append(grads[2])
        up_grads.append(grads[3])
        act_grads.append(grads[4])
        down_grads.append(grads[5])
    empty = jnp.zeros((1, NI * NJ, D), jnp.bfloat16)
    next_input = jnp.concatenate([empty, jnp.stack(forward_outs[:-1])], axis=0)
    upstream_grad = jnp.concatenate([jnp.stack(input_grads[1:]), empty], axis=0)
    return (next_input, upstream_grad, jnp.stack(kernel_grads), jnp.stack(mix_grads), jnp.stack(up_grads), jnp.stack(act_grads), jnp.stack(down_grads))
```

```python
import functools
import math

import jax
import jax.numpy as jnp
from jax import lax
from jax.experimental import pallas as pl
from jax.experimental.pallas import tpu as pltpu
from jax.sharding import PartitionSpec as P

NB = 4
EPS = 1e-06
F32 = jnp.float32
BF16 = jnp.bfloat16
MIB = 1024 * 1024


def dot(a, b):
    return jnp.dot(a, b, preferred_element_type=F32)


def dot_t(a, b):
    return lax.dot_general(a, b, (((1,), (1,)), ((), ())), preferred_element_type=F32)


def t_dot(a, b):
    return lax.dot_general(a, b, (((0,), (0,)), ((), ())), preferred_element_type=F32)


def rms_scale(v):
    return lax.rsqrt(jnp.mean(v * v, axis=-1, keepdims=True) + EPS)


def norm_back(v, scale, gain, grad):
    scaled = gain * grad
    return scale * scaled - v * (scale * scale * scale) * jnp.mean(
        scaled * v, axis=-1, keepdims=True
    )


def cols_of(array, b, width):
    return array[:, b * width : (b + 1) * width]


def params(mib, steps=1):
    return pltpu.CompilerParams(
        dimension_semantics=("arbitrary",) * steps, vmem_limit_bytes=mib * MIB
    )


def cost(flops, nbytes):
    return pl.CostEstimate(flops=int(flops), bytes_accessed=int(nbytes), transcendentals=0)


class Sizes:
    def __init__(self, n, rows, cols, width):
        self.n = n
        self.rows = rows
        self.cols = cols
        self.width = width
        self.line = n * cols
        self.tall = n * rows
        self.tokens = rows * self.line
        self.per = 2 if rows % 2 == 0 else 1
        self.aligned = cols % 16 == 0

    def sent_shape(self):
        if self.aligned:
            return (self.n, self.rows, self.cols, self.width)
        return (self.rows, self.line, self.width)

    def sent_spec(self):
        if self.aligned:
            return pl.BlockSpec(
                (self.n, self.per, self.cols, self.width), lambda i: (0, i, 0, 0)
            )
        return pl.BlockSpec((self.per, self.line, self.width), lambda i: (i, 0, 0))

    def put(self, ref, r, value):
        if self.aligned:
            ref[:, r] = value.reshape(self.n, self.cols, self.width)
        else:
            ref[r] = value

    def get(self, ref, r):
        if self.aligned:
            return ref[:, r].reshape(self.line, self.width)
        return ref[r]

    def to_columns(self, array):
        if not self.aligned:
            array = array.reshape(self.rows, self.n, self.cols, self.width).transpose(1, 0, 2, 3)
        array = lax.all_to_all(array, "seq", split_axis=0, concat_axis=0, tiled=True)
        return array.reshape(self.tall * self.cols, self.width)

    def to_rows(self, array):
        array = array.reshape(self.n, self.rows, self.cols, self.width)
        array = lax.all_to_all(array, "seq", split_axis=0, concat_axis=0, tiled=True)
        if not self.aligned:
            array = array.transpose(1, 0, 2, 3).reshape(self.rows, self.line, self.width)
        return array

    def token_spec(self, width):
        return pl.BlockSpec((self.per * self.line, width), lambda i: (i, 0))

    def factor_spec(self):
        return pl.BlockSpec((self.per, self.line, self.line), lambda i: (i, 0, 0))


def whole(shape):
    return pl.BlockSpec(shape, lambda i: (0,) * len(shape))


def front_kernel(sz, x_ref, gain_ref, first_ref, sent_ref):
    for r in range(sz.per):
        x = x_ref[pl.ds(r * sz.line, sz.line), :].astype(F32)
        normed = (x * rms_scale(x) * gain_ref[...]).astype(BF16)
        sz.put(sent_ref, r, dot(first_ref[r], normed).astype(BF16))


def front(sz, x, gain, first):
    return pl.pallas_call(
        functools.partial(front_kernel, sz),
        grid=(sz.rows // sz.per,),
        in_specs=[sz.token_spec(sz.width), whole((1, sz.width)), sz.factor_spec()],
        out_specs=sz.sent_spec(),
        out_shape=jax.ShapeDtypeStruct(sz.sent_shape(), BF16),
        compiler_params=params(16),
        cost_estimate=cost(2 * sz.tokens * sz.line * sz.width, 4 * sz.tokens * sz.width),
        name="front",
    )(x, gain, first)


def expand_kernel(cols, tall, thin_ref, wide_ref):
    size = tall * cols
    pick = lax.broadcasted_iota(jnp.int32, (tall, size), 1) // cols
    pick = (pick == lax.broadcasted_iota(jnp.int32, (tall, size), 0)).astype(F32).astype(BF16)
    spread = dot(thin_ref[0], pick)
    left = lax.broadcasted_iota(jnp.int32, (size, size), 0) % cols
    right = lax.broadcasted_iota(jnp.int32, (size, size), 1) % cols
    wide_ref[0] = jnp.where(left == right, spread, 0.0).astype(BF16)


def expand(sz, second, third):
    size = sz.tall * sz.cols
    thin = jnp.stack(
        [
            second.transpose(1, 0, 2).reshape(size, sz.tall),
            third.transpose(1, 0, 2).reshape(size, sz.tall),
            third.transpose(2, 0, 1).reshape(size, sz.tall),
            second.transpose(2, 0, 1).reshape(size, sz.tall),
        ]
    )
    return pl.pallas_call(
        functools.partial(expand_kernel, sz.cols, sz.tall),
        grid=(4,),
        in_specs=[pl.BlockSpec((1, size, sz.tall), lambda i: (i, 0, 0))],
        out_specs=pl.BlockSpec((1, size, size), lambda i: (i, 0, 0)),
        out_shape=jax.ShapeDtypeStruct((4, size, size), BF16),
        compiler_params=params(32),
        cost_estimate=cost(8 * size * size * sz.tall, 8 * size * size),
        name="expand",
    )(thin)


def middle_kernel(x_ref, second_ref, third_ref, spectrum_ref, out_ref, *mixed_ref):
    mixed = dot(second_ref[0], x_ref[...])
    if mixed_ref:
        mixed_ref[0][...] = mixed
    filtered = (mixed * spectrum_ref[...].astype(F32)).astype(BF16)
    out_ref[...] = dot(third_ref[0], filtered).astype(BF16)


def middle(sz, x, wide, spectrum, keep):
    size = sz.tall * sz.cols
    part = 256
    strip = pl.BlockSpec((size, part), lambda i: (0, i))
    shapes = [jax.ShapeDtypeStruct((size, sz.width), BF16)]
    if keep:
        shapes.append(jax.ShapeDtypeStruct((size, sz.width), F32))
    return pl.pallas_call(
        middle_kernel,
        grid=(sz.width // part,),
        in_specs=[
            strip,
            pl.BlockSpec((1, size, size), lambda i: (0, 0, 0)),
            pl.BlockSpec((1, size, size), lambda i: (1, 0, 0)),
            strip,
        ],
        out_specs=[strip] * len(shapes),
        out_shape=shapes,
        compiler_params=params(28),
        cost_estimate=cost(4 * size * size * sz.width, 10 * size * sz.width),
        name="middle",
    )(x, wide, wide, spectrum)


def middle_back_kernel(
    d_ref, third_ref, second_ref, spectrum_ref, mixed_ref, out_ref, grad_ref
):
    d_filtered = dot(third_ref[0], d_ref[...])
    grad_ref[...] = (d_filtered * mixed_ref[...]).astype(BF16)
    d_mixed = (d_filtered * spectrum_ref[...].astype(F32)).astype(BF16)
    out_ref[...] = dot(second_ref[0], d_mixed).astype(BF16)


def middle_back(sz, d, wide, spectrum, mixed):
    size = sz.tall * sz.cols
    part = 256
    strip = pl.BlockSpec((size, part), lambda i: (0, i))
    return pl.pallas_call(
        middle_back_kernel,
        grid=(sz.width // part,),
        in_specs=[
            strip,
            pl.BlockSpec((1, size, size), lambda i: (2, 0, 0)),
            pl.BlockSpec((1, size, size), lambda i: (3, 0, 0)),
            strip,
            strip,
        ],
        out_specs=[strip, strip],
        out_shape=[jax.ShapeDtypeStruct((size, sz.width), BF16)] * 2,
        compiler_params=params(28),
        cost_estimate=cost(4 * size * size * sz.width, 12 * size * sz.width),
        name="middle_back",
    )(d, wide, wide, spectrum, mixed)


def tail_front(sz, x_ref, b1_ref, fourth_ref, gain_one, mix_ref):
    x = x_ref[...].astype(F32)
    normed = (x * rms_scale(x) * gain_one).astype(BF16)
    collected = [dot(fourth_ref[r], sz.get(b1_ref, r)) for r in range(sz.per)]
    back = collected[0] if sz.per == 1 else jnp.concatenate(collected, axis=0)
    wide = sz.width // NB
    gate = jnp.concatenate(
        [
            dot(cols_of(normed, b, wide), mix_ref[b * wide : (b + 1) * wide, :])
            for b in range(NB)
        ],
        axis=1,
    )
    y1 = (x + back * gate).astype(BF16)
    return normed, back, gate, y1


def tail_kernel(
    sz,
    x_ref,
    b1_ref,
    fourth_ref,
    gain_one_ref,
    gain_two_ref,
    mix_ref,
    up_ref,
    act_ref,
    down_ref,
    out_ref,
):
    _, _, _, y1 = tail_front(sz, x_ref, b1_ref, fourth_ref, gain_one_ref[...], mix_ref)
    y = y1.astype(F32)
    n2 = (y * rms_scale(y) * gain_two_ref[...]).astype(BF16)
    wide = sz.width // NB
    hidden = []
    for b in range(NB):
        rows = slice(b * wide, (b + 1) * wide)
        lifted = dot(n2[:, rows], up_ref[rows, :])
        gated = dot(n2[:, rows], act_ref[rows, :])
        hidden.append((gated * jax.nn.sigmoid(gated) * lifted).astype(BF16))
    units = hidden[0].shape[1]
    piece = units // NB
    for b in range(NB):
        mixed = jnp.concatenate([cols_of(h, b, piece) for h in hidden], axis=1)
        out_ref[:, b * wide : (b + 1) * wide] = (
            cols_of(y, b, wide) + dot(mixed, down_ref[b * units : (b + 1) * units, :])
        ).astype(BF16)


def tail_specs(sz, weights):
    return [
        sz.token_spec(sz.width),
        sz.sent_spec(),
        sz.factor_spec(),
        whole((1, sz.width)),
        whole((1, sz.width)),
    ] + [whole(w.shape) for w in weights]


def tail(sz, x, b1, fourth, gain_one, gain_two, *weights):
    return pl.pallas_call(
        functools.partial(tail_kernel, sz),
        grid=(sz.rows // sz.per,),
        in_specs=tail_specs(sz, weights),
        out_specs=sz.token_spec(sz.width),
        out_shape=jax.ShapeDtypeStruct((sz.tokens, sz.width), BF16),
        compiler_params=params(40),
        cost_estimate=cost(8 * sz.tokens * sz.width * sz.width // 2, 8 * sz.tokens * sz.width),
        name="tail",
    )(x, b1, fourth, gain_one, gain_two, *weights)


def turn_kernel(
    sz,
    x_ref,
    b1_ref,
    fourth_ref,
    gain_one_ref,
    gain_two_ref,
    mix_ref,
    up_ref,
    act_ref,
    down_ref,
    g_ref,
    sent_ref,
    dy_ref,
    dgate_ref,
    n1_ref,
    n2_ref,
    hs_ref,
    dup_ref,
    dact_ref,
):
    n1, back, gate, y1 = tail_front(sz, x_ref, b1_ref, fourth_ref, gain_one_ref[...], mix_ref)
    n1_ref[...] = n1
    y = y1.astype(F32)
    scale_two = rms_scale(y)
    n2 = (y * scale_two * gain_two_ref[...]).astype(BF16)
    n2_ref[...] = n2
    wide = sz.width // NB
    units = up_ref.shape[1]
    piece = units // NB
    d_shuffled = [
        dot_t(g_ref[:, b * wide : (b + 1) * wide], down_ref[b * units : (b + 1) * units, :]).astype(
            BF16
        )
        for b in range(NB)
    ]
    d_n2 = []
    for b in range(NB):
        rows = slice(b * wide, (b + 1) * wide)
        lifted = dot(n2[:, rows], up_ref[rows, :])
        gated = dot(n2[:, rows], act_ref[rows, :])
        sigma = jax.nn.sigmoid(gated)
        silu = gated * sigma
        hidden = (silu * lifted).astype(BF16)
        for k in range(NB):
            at = k * units + b * piece
            hs_ref[:, at : at + piece] = cols_of(hidden, k, piece)
        d_hidden = jnp.concatenate([cols_of(d, b, piece) for d in d_shuffled], axis=1).astype(F32)
        d_lift = (d_hidden * silu).astype(BF16)
        d_gated = (d_hidden * lifted * sigma * (1.0 + gated * (1.0 - sigma))).astype(BF16)
        dup_ref[:, b * units : (b + 1) * units] = d_lift
        dact_ref[:, b * units : (b + 1) * units] = d_gated
        d_n2.append(dot_t(d_lift, up_ref[rows, :]) + dot_t(d_gated, act_ref[rows, :]))
    d_n2 = jnp.concatenate(d_n2, axis=1)
    dy = (g_ref[...].astype(F32) + norm_back(y, scale_two, gain_two_ref[...], d_n2)).astype(BF16)
    dy_ref[...] = dy
    dyw = dy.astype(F32)
    dgate_ref[...] = (dyw * back).astype(BF16)
    d_back = (dyw * gate).astype(BF16)
    for r in range(sz.per):
        part = d_back[r * sz.line : (r + 1) * sz.line, :]
        sz.put(sent_ref, r, t_dot(fourth_ref[r], part).astype(BF16))


def turn(sz, x, b1, fourth, gain_one, gain_two, mix, up, act, down, g):
    weights = (mix, up, act, down)
    units = NB * up.shape[1]
    widths = [sz.width] * 4 + [units] * 3
    return pl.pallas_call(
        functools.partial(turn_kernel, sz),
        grid=(sz.rows // sz.per,),
        in_specs=tail_specs(sz, weights) + [sz.token_spec(sz.width)],
        out_specs=[sz.sent_spec()] + [sz.token_spec(w) for w in widths],
        out_shape=[jax.ShapeDtypeStruct(sz.sent_shape(), BF16)]
        + [jax.ShapeDtypeStruct((sz.tokens, w), BF16) for w in widths],
        compiler_params=params(48),
        cost_estimate=cost(8 * sz.tokens * sz.width * sz.width, 30 * sz.tokens * sz.width),
        name="turn",
    )(x, b1, fourth, gain_one, gain_two, *weights, g)


def weights_kernel(factor, share, n1, dgate, n2, dup, dact, hs, g, out_ref):
    wide = n1.shape[1]
    units = dup.shape[1]
    out_ref[:, :wide] = (t_dot(n1[...], dgate[...]) * factor).astype(BF16)
    out_ref[:, wide : wide + units] = (t_dot(n2[...], dup[...]) * factor).astype(BF16)
    out_ref[:, wide + units : wide + 2 * units] = (t_dot(n2[...], dact[...]) * factor).astype(BF16)
    down = (t_dot(hs[...], g[...]) * factor).astype(BF16)
    ratio = units // wide
    for k in range(units // share):
        at = wide + 2 * units + (k % ratio) * wide
        out_ref[(k // ratio) * share : (k // ratio + 1) * share, at : at + wide] = down[
            k * share : (k + 1) * share, :
        ]


def weight_grads(sz, factor, n1, dgate, n2, dup, dact, hs, g):
    wide = sz.width // NB
    units = dup.shape[1] // NB
    total = wide + 3 * units
    slim = pl.BlockSpec((sz.tokens, wide), lambda i: (0, i))
    broad = pl.BlockSpec((sz.tokens, units), lambda i: (0, i))
    return pl.pallas_call(
        functools.partial(weights_kernel, factor, sz.width // sz.n),
        grid=(NB,),
        in_specs=[slim, slim, slim, broad, broad, broad, slim],
        out_specs=pl.BlockSpec((wide, total), lambda i: (i, 0)),
        out_shape=jax.ShapeDtypeStruct((sz.width, total), BF16),
        compiler_params=params(32),
        cost_estimate=cost(2 * sz.tokens * sz.width * total, 24 * sz.tokens * sz.width),
        name="weight_grads",
    )(n1, dgate, n2, dup, dact, hs, g)


def last_kernel(sz, x_ref, d_ref, first_ref, gain_ref, mix_ref, dgate_ref, dy_ref, out_ref):
    wide = sz.width // NB
    gain = gain_ref[...]
    for r in range(sz.per):
        at = pl.ds(r * sz.line, sz.line)
        gated = jnp.concatenate(
            [
                dot_t(
                    dgate_ref[at, b * wide : (b + 1) * wide], mix_ref[b * wide : (b + 1) * wide, :]
                )
                for b in range(NB)
            ],
            axis=1,
        )
        d_normed = t_dot(first_ref[r], sz.get(d_ref, r)) + gated
        x = x_ref[at, :].astype(F32)
        out_ref[at, :] = (
            dy_ref[at, :].astype(F32) + norm_back(x, rms_scale(x), gain, d_normed)
        ).astype(BF16)


def last(sz, x, d, first, gain, mix, dgate, dy):
    tokens = sz.token_spec(sz.width)
    return pl.pallas_call(
        functools.partial(last_kernel, sz),
        grid=(sz.rows // sz.per,),
        in_specs=[
            tokens,
            sz.sent_spec(),
            sz.factor_spec(),
            whole((1, sz.width)),
            whole(mix.shape),
            tokens,
            tokens,
        ],
        out_specs=tokens,
        out_shape=jax.ShapeDtypeStruct((sz.tokens, sz.width), BF16),
        compiler_params=params(20),
        cost_estimate=cost(2 * sz.tokens * sz.width * 384, 10 * sz.tokens * sz.width),
        name="last",
    )(x, d, first, gain, mix, dgate, dy)


def shift(array, by):
    length = lax.axis_size("section")
    pairs = [(i, i + by) for i in range(length) if 0 <= i + by < length]
    return lax.ppermute(array, "section", pairs)


def shards(
    section_input,
    stashed_input,
    output_grad,
    gain_mixer,
    gain_channel,
    factor_first,
    factor_second,
    spectrum,
    factor_third,
    factor_fourth,
    mixer_gate,
    channel_up,
    channel_gate,
    channel_down,
):
    first = factor_first[0]
    fourth = factor_fourth[0]
    n = lax.axis_size("seq")
    rows = first.shape[0]
    cols = factor_second.shape[1]
    width = section_input.shape[2]
    sz = Sizes(n, rows, cols, width)
    size = sz.tall * cols
    kernel_here = spectrum[0].reshape(size, width)
    mix, up, act, down = mixer_gate[0], channel_up[0], channel_gate[0], channel_down[0]
    gain_one, gain_two = gain_mixer, gain_channel
    xa, xb, g = section_input[0], stashed_input[0], output_grad[0]
    factor = 1.0 / math.sqrt(sz.tall * sz.line)

    recv_b = sz.to_columns(front(sz, xb, gain_one, first))
    wide = expand(sz, factor_second[0], factor_third[0])
    sent_a = front(sz, xa, gain_one, first)
    sent_a, recv_b = lax.optimization_barrier((sent_a, recv_b))
    recv_a = sz.to_columns(sent_a)
    out_b, mixed_b = middle(sz, recv_b, wide, kernel_here, True)
    out_b, recv_a = lax.optimization_barrier((out_b, recv_a))
    rows_b = sz.to_rows(out_b)
    (out_a,) = middle(sz, recv_a, wide, kernel_here, False)
    out_a, rows_b = lax.optimization_barrier((out_a, rows_b))
    rows_a = sz.to_rows(out_a)

    sent, dy, dgate, n1, n2, hs, dup, dact = turn(
        sz, xb, rows_b, fourth, gain_one, gain_two, mix, up, act, down, g
    )
    sent, rows_a = lax.optimization_barrier((sent, rows_a))
    d_cols = sz.to_columns(sent)
    next_input = shift(tail(sz, xa, rows_a, fourth, gain_one, gain_two, mix, up, act, down), 1)
    grads = weight_grads(sz, factor, n1, dgate, n2, dup, dact, hs, g)
    d_out, spectrum_grad = middle_back(sz, d_cols, wide, kernel_here, mixed_b)
    d_rows = sz.to_rows(d_out)
    grads, d_rows = lax.optimization_barrier((grads, d_rows))
    upstream = shift(last(sz, xb, d_rows, first, gain_one, mix, dgate, dy), -1)
    grads = lax.psum_scatter(grads, "seq", scatter_dimension=0, tiled=True)
    w, u = width // NB, up.shape[1]
    down_grad = jnp.concatenate(
        [grads[:, w + 2 * u + k * w : w + 2 * u + (k + 1) * w] for k in range(u // w)], axis=0
    )
    return (
        next_input[None],
        upstream[None],
        spectrum_grad.reshape(spectrum.shape),
        grads[None, :, :w],
        grads[None, :, w : w + u],
        grads[None, :, w + u : w + 2 * u],
        down_grad[None],
    )


def solution(mesh):
    in_specs = (
        P("section", "seq", None),
        P("section", "seq", None),
        P("section", "seq", None),
        P("section", None),
        P("section", None),
        P("section", "seq", None, None),
        P("section", "seq", None, None),
        P("section", None, "seq", None),
        P("section", "seq", None, None),
        P("section", "seq", None, None),
        P("section", None, None),
        P("section", None, None),
        P("section", None, None),
        P("section", None, None),
    )
    out_specs = (
        P("section", "seq", None),
        P("section", "seq", None),
        P("section", None, "seq", None),
        P("section", "seq", None),
        P("section", "seq", None),
        P("section", "seq", None),
        P("section", "seq", None),
    )
    return jax.shard_map(shards, mesh=mesh, in_specs=in_specs, out_specs=out_specs, check_vma=False)
```

```python
import functools
import math

import jax
import jax.numpy as jnp
from jax import lax
from jax.experimental import pallas as pl
from jax.experimental.pallas import tpu as pltpu
from jax.sharding import PartitionSpec as P

NB = 4
EPS = 1e-06
F32 = jnp.float32
BF16 = jnp.bfloat16
VMEM = 56 * 1024 * 1024


def dot(a, b):
    return jnp.dot(a, b, preferred_element_type=F32)


def dot_t(a, b):
    return lax.dot_general(a, b, (((1,), (1,)), ((), ())), preferred_element_type=F32)


def t_dot(a, b):
    return lax.dot_general(a, b, (((0,), (0,)), ((), ())), preferred_element_type=F32)


def rms_scale(v):
    return lax.rsqrt(jnp.mean(v * v, axis=-1, keepdims=True) + EPS)


def norm_back(v, scale, gain, grad):
    scaled = gain * grad
    return scale * scaled - v * (scale * scale * scale) * jnp.mean(
        scaled * v, axis=-1, keepdims=True
    )


def cols_of(array, b, width):
    return array[:, b * width : (b + 1) * width]


def call(body, grid, in_specs, out_specs, out_shape, price, name, *args):
    return pl.pallas_call(
        body,
        grid=(grid,),
        in_specs=in_specs,
        out_specs=out_specs,
        out_shape=out_shape,
        compiler_params=pltpu.CompilerParams(
            dimension_semantics=("arbitrary",), vmem_limit_bytes=VMEM
        ),
        cost_estimate=price,
        name=name,
    )(*args)


def call_exchanging(
    sz, send, span, cid, body, grid, in_specs, out_specs, out_shape, price, name, *args
):
    n = sz.n
    count = len(in_specs)

    def kernel(send_ref, *refs):
        ins, recv_ref = refs[:count], refs[count]
        outs = refs[count + 1 : -3]
        send_sem, recv_sem, own_sem = refs[-3:]
        step = pl.program_id(0)
        me = lax.axis_index("seq")

        def copies():
            own = pltpu.make_async_copy(
                send_ref.at[me, pl.ds(span[0], span[1])], recv_ref.at[me], own_sem
            )
            far = [
                pltpu.make_async_remote_copy(
                    src_ref=send_ref.at[lax.rem(me + k, n), pl.ds(span[0], span[1])],
                    dst_ref=recv_ref.at[me],
                    send_sem=send_sem.at[k - 1],
                    recv_sem=recv_sem.at[k - 1],
                    device_id={"seq": lax.rem(me + k, n)},
                    device_id_type=pl.DeviceIdType.MESH,
                )
                for k in range(1, n)
            ]
            return far + [own]

        @pl.when(step == 0)
        def _():
            barrier = pltpu.get_barrier_semaphore()
            for k in range(1, n):
                pl.semaphore_signal(
                    barrier,
                    inc=1,
                    device_id={"seq": lax.rem(me + k, n)},
                    device_id_type=pl.DeviceIdType.MESH,
                )
            pl.semaphore_wait(barrier, n - 1)
            for copy in copies():
                copy.start()

        body(*ins, *outs)

        @pl.when(step == grid - 1)
        def _():
            for copy in copies():
                copy.wait()

    shape = (n, span[1]) + send.shape[2:]
    return pl.pallas_call(
        kernel,
        grid=(grid,),
        in_specs=[pl.BlockSpec(memory_space=pl.ANY)] + in_specs,
        out_specs=[pl.BlockSpec(memory_space=pl.ANY)] + out_specs,
        out_shape=[jax.ShapeDtypeStruct(shape, send.dtype)] + out_shape,
        scratch_shapes=[
            pltpu.SemaphoreType.DMA((n - 1,)),
            pltpu.SemaphoreType.DMA((n - 1,)),
            pltpu.SemaphoreType.DMA(()),
        ],
        compiler_params=pltpu.CompilerParams(
            dimension_semantics=("arbitrary",),
            vmem_limit_bytes=VMEM,
            collective_id=cid,
            has_side_effects=True,
        ),
        cost_estimate=price,
        name=name,
    )(send, *args)


def cost(flops, nbytes):
    return pl.CostEstimate(flops=int(flops), bytes_accessed=int(nbytes), transcendentals=0)


class Sizes:
    def __init__(self, n, rows, cols, width):
        self.n = n
        self.rows = rows
        self.cols = cols
        self.width = width
        self.line = n * cols
        self.tall = n * rows
        self.tokens = rows * self.line
        self.per = 2 if rows % 2 == 0 else 1
        self.aligned = cols % 16 == 0
        self.groups = cols // 8 if cols % 8 == 0 else 1

    def sent_shape(self):
        if self.aligned:
            return (self.n, self.rows, self.cols, self.width)
        return (self.rows, self.line, self.width)

    def sent_spec(self):
        if self.aligned:
            return pl.BlockSpec(
                (self.n, self.per, self.cols, self.width), lambda i: (0, i, 0, 0)
            )
        return pl.BlockSpec((self.per, self.line, self.width), lambda i: (i, 0, 0))

    def put(self, ref, r, value):
        if self.aligned:
            ref[:, r] = value.reshape(self.n, self.cols, self.width)
        else:
            ref[r] = value

    def get(self, ref, r):
        if self.aligned:
            return ref[:, r].reshape(self.line, self.width)
        return ref[r]

    def to_send(self, array):
        if self.aligned:
            return array
        return array.reshape(self.rows, self.n, self.cols, self.width).transpose(1, 0, 2, 3)

    def to_flat(self, array):
        return array.reshape(self.tall * self.cols, self.width)

    def from_flat(self, array):
        return array.reshape(self.n, self.rows, self.cols, self.width)

    def to_rows(self, array):
        if self.aligned:
            return array
        return array.transpose(1, 0, 2, 3).reshape(-1, self.line, self.width)

    def token_spec(self, width, skip=0):
        return pl.BlockSpec((self.per * self.line, width), lambda i: (i + skip, 0))

    def factor_spec(self, skip=0):
        return pl.BlockSpec((self.per, self.line, self.line), lambda i: (i + skip, 0, 0))


def whole(shape):
    return pl.BlockSpec(shape, lambda i: (0,) * len(shape))


def front_kernel(sz, x_ref, gain_ref, first_ref, sent_ref):
    for r in range(sz.per):
        x = x_ref[pl.ds(r * sz.line, sz.line), :].astype(F32)
        normed = (x * rms_scale(x) * gain_ref[...]).astype(BF16)
        sz.put(sent_ref, r, dot(first_ref[r], normed).astype(BF16))


def front_parts(sz, x, gain, first):
    return (
        functools.partial(front_kernel, sz),
        sz.rows // sz.per,
        [sz.token_spec(sz.width), whole((1, sz.width)), sz.factor_spec()],
        [sz.sent_spec()],
        [jax.ShapeDtypeStruct(sz.sent_shape(), BF16)],
        cost(2 * sz.tokens * sz.line * sz.width, 4 * sz.tokens * sz.width),
        "front",
        x,
        gain,
        first,
    )


def expand_kernel(cols, tall, thin_ref, wide_ref):
    size = tall * cols
    pick = lax.broadcasted_iota(jnp.int32, (tall, size), 1) // cols
    pick = (pick == lax.broadcasted_iota(jnp.int32, (tall, size), 0)).astype(F32).astype(BF16)
    left = lax.broadcasted_iota(jnp.int32, (size, size), 0) % cols
    right = lax.broadcasted_iota(jnp.int32, (size, size), 1) % cols
    for g in range(thin_ref.shape[1]):
        spread = dot(thin_ref[0, g], pick)
        wide_ref[0, g] = jnp.where(left == right, spread, 0.0).astype(BF16)


def expand(sz, second, third):
    inner = sz.cols // sz.groups
    size = sz.tall * inner

    def thin(factor, order):
        grouped = factor.reshape(sz.groups, inner, sz.tall, sz.tall)
        return grouped.transpose(order).reshape(sz.groups, size, sz.tall)

    ahead, back = (0, 2, 1, 3), (0, 3, 1, 2)
    stack = jnp.stack(
        [thin(second, ahead), thin(third, ahead), thin(third, back), thin(second, back)]
    )
    return call(
        functools.partial(expand_kernel, inner, sz.tall),
        4,
        [pl.BlockSpec((1, sz.groups, size, sz.tall), lambda i: (i, 0, 0, 0))],
        pl.BlockSpec((1, sz.groups, size, size), lambda i: (i, 0, 0, 0)),
        jax.ShapeDtypeStruct((4, sz.groups, size, size), BF16),
        cost(8 * sz.groups * size * size * sz.tall, 8 * sz.groups * size * size),
        "expand",
        stack,
    )


def mix_rows(sz, wide_ref, x):
    if sz.groups == 1:
        return dot(wide_ref[0, 0], x.astype(BF16))
    part = x.shape[1]
    inner = sz.cols // sz.groups
    x = x.reshape(sz.tall, sz.cols, part)
    outs = []
    for g in range(sz.groups):
        piece = x[:, g * inner : (g + 1) * inner].reshape(sz.tall * inner, part).astype(BF16)
        outs.append(dot(wide_ref[0, g], piece).reshape(sz.tall, inner, part))
    return jnp.concatenate(outs, axis=1).reshape(sz.tall * sz.cols, part)


def middle_kernel(sz, x_ref, second_ref, third_ref, spectrum_ref, out_ref, *mixed_ref):
    mixed = mix_rows(sz, second_ref, x_ref[...].astype(F32))
    if mixed_ref:
        mixed_ref[0][...] = mixed
    filtered = mixed * spectrum_ref[...].astype(F32)
    out_ref[...] = mix_rows(sz, third_ref, filtered).astype(BF16)


def wide_spec(wide, which):
    return pl.BlockSpec((1,) + wide.shape[1:], lambda i: (which, 0, 0, 0))


def middle_parts(sz, x, wide, spectrum, keep):
    size = sz.tall * sz.cols
    part = 256
    strip = pl.BlockSpec((size, part), lambda i: (0, i))
    shapes = [jax.ShapeDtypeStruct((size, sz.width), BF16)]
    if keep:
        shapes.append(jax.ShapeDtypeStruct((size, sz.width), F32))
    return (
        functools.partial(middle_kernel, sz),
        sz.width // part,
        [strip, wide_spec(wide, 0), wide_spec(wide, 1), strip],
        [strip] * len(shapes),
        shapes,
        cost(4 * size * size * sz.width // sz.groups, 10 * size * sz.width),
        "middle",
        x,
        wide,
        wide,
        spectrum,
    )


def middle_back_kernel(
    sz, d_ref, third_ref, second_ref, spectrum_ref, mixed_ref, out_ref, grad_ref
):
    d_filtered = mix_rows(sz, third_ref, d_ref[...].astype(F32))
    grad_ref[...] = (d_filtered * mixed_ref[...]).astype(BF16)
    d_mixed = d_filtered * spectrum_ref[...].astype(F32)
    out_ref[...] = mix_rows(sz, second_ref, d_mixed).astype(BF16)


def middle_back(sz, d, wide, spectrum, mixed):
    size = sz.tall * sz.cols
    part = 256
    strip = pl.BlockSpec((size, part), lambda i: (0, i))
    return call(
        functools.partial(middle_back_kernel, sz),
        sz.width // part,
        [strip, wide_spec(wide, 2), wide_spec(wide, 3), strip, strip],
        [strip, strip],
        [jax.ShapeDtypeStruct((size, sz.width), BF16)] * 2,
        cost(4 * size * size * sz.width // sz.groups, 12 * size * sz.width),
        "middle_back",
        d,
        wide,
        wide,
        spectrum,
        mixed,
    )


def tail_front(sz, x_ref, b1_ref, fourth_ref, gain_one, mix_ref):
    x = x_ref[...].astype(F32)
    normed = (x * rms_scale(x) * gain_one).astype(BF16)
    collected = [dot(fourth_ref[r], sz.get(b1_ref, r)) for r in range(sz.per)]
    back = collected[0] if sz.per == 1 else jnp.concatenate(collected, axis=0)
    wide = sz.width // NB
    gate = jnp.concatenate(
        [
            dot(cols_of(normed, b, wide), mix_ref[b * wide : (b + 1) * wide, :])
            for b in range(NB)
        ],
        axis=1,
    )
    y1 = (x + back * gate).astype(BF16)
    return normed, back, gate, y1


def tail_kernel(
    sz,
    x_ref,
    b1_ref,
    fourth_ref,
    gain_one_ref,
    gain_two_ref,
    mix_ref,
    up_ref,
    act_ref,
    down_ref,
    out_ref,
):
    _, _, _, y1 = tail_front(sz, x_ref, b1_ref, fourth_ref, gain_one_ref[...], mix_ref)
    y = y1.astype(F32)
    n2 = (y * rms_scale(y) * gain_two_ref[...]).astype(BF16)
    wide = sz.width // NB
    hidden = []
    for b in range(NB):
        rows = slice(b * wide, (b + 1) * wide)
        lifted = dot(n2[:, rows], up_ref[rows, :])
        gated = dot(n2[:, rows], act_ref[rows, :])
        hidden.append((gated * jax.nn.sigmoid(gated) * lifted).astype(BF16))
    units = hidden[0].shape[1]
    piece = units // NB
    for b in range(NB):
        mixed = jnp.concatenate([cols_of(h, b, piece) for h in hidden], axis=1)
        out_ref[:, b * wide : (b + 1) * wide] = (
            cols_of(y, b, wide) + dot(mixed, down_ref[b * units : (b + 1) * units, :])
        ).astype(BF16)


def tail_specs(sz, weights):
    return [
        sz.token_spec(sz.width),
        sz.sent_spec(),
        sz.factor_spec(),
        whole((1, sz.width)),
        whole((1, sz.width)),
    ] + [whole(w.shape) for w in weights]


def tail_parts(sz, x, b1, fourth, gain_one, gain_two, *weights):
    return (
        functools.partial(tail_kernel, sz),
        sz.rows // sz.per,
        tail_specs(sz, weights),
        [sz.token_spec(sz.width)],
        [jax.ShapeDtypeStruct((sz.tokens, sz.width), BF16)],
        cost(4 * sz.tokens * sz.width * sz.width, 8 * sz.tokens * sz.width),
        "tail",
        x,
        b1,
        fourth,
        gain_one,
        gain_two,
        *weights,
    )


def turn_kernel(
    sz,
    x_ref,
    b1_ref,
    fourth_ref,
    gain_one_ref,
    gain_two_ref,
    mix_ref,
    up_ref,
    act_ref,
    down_ref,
    g_ref,
    sent_ref,
    dy_ref,
    dgate_ref,
    n1_ref,
    n2_ref,
    hs_ref,
    dup_ref,
    dact_ref,
):
    n1, back, gate, y1 = tail_front(sz, x_ref, b1_ref, fourth_ref, gain_one_ref[...], mix_ref)
    n1_ref[...] = n1
    y = y1.astype(F32)
    scale_two = rms_scale(y)
    n2 = (y * scale_two * gain_two_ref[...]).astype(BF16)
    n2_ref[...] = n2
    wide = sz.width // NB
    units = up_ref.shape[1]
    piece = units // NB
    d_shuffled = [
        dot_t(g_ref[:, b * wide : (b + 1) * wide], down_ref[b * units : (b + 1) * units, :]).astype(
            BF16
        )
        for b in range(NB)
    ]
    d_n2 = []
    for b in range(NB):
        rows = slice(b * wide, (b + 1) * wide)
        lifted = dot(n2[:, rows], up_ref[rows, :])
        gated = dot(n2[:, rows], act_ref[rows, :])
        sigma = jax.nn.sigmoid(gated)
        silu = gated * sigma
        hidden = (silu * lifted).astype(BF16)
        for k in range(NB):
            at = k * units + b * piece
            hs_ref[:, at : at + piece] = cols_of(hidden, k, piece)
        d_hidden = jnp.concatenate([cols_of(d, b, piece) for d in d_shuffled], axis=1).astype(F32)
        d_lift = (d_hidden * silu).astype(BF16)
        d_gated = (d_hidden * lifted * sigma * (1.0 + gated * (1.0 - sigma))).astype(BF16)
        dup_ref[:, b * units : (b + 1) * units] = d_lift
        dact_ref[:, b * units : (b + 1) * units] = d_gated
        d_n2.append(dot_t(d_lift, up_ref[rows, :]) + dot_t(d_gated, act_ref[rows, :]))
    d_n2 = jnp.concatenate(d_n2, axis=1)
    dy = (g_ref[...].astype(F32) + norm_back(y, scale_two, gain_two_ref[...], d_n2)).astype(BF16)
    dy_ref[...] = dy
    dyw = dy.astype(F32)
    dgate_ref[...] = (dyw * back).astype(BF16)
    d_back = (dyw * gate).astype(BF16)
    for r in range(sz.per):
        part = d_back[r * sz.line : (r + 1) * sz.line, :]
        sz.put(sent_ref, r, t_dot(fourth_ref[r], part).astype(BF16))


def turn_parts(sz, x, b1, fourth, gain_one, gain_two, mix, up, act, down, g):
    weights = (mix, up, act, down)
    units = NB * up.shape[1]
    widths = [sz.width] * 4 + [units] * 3
    return (
        functools.partial(turn_kernel, sz),
        sz.rows // sz.per,
        tail_specs(sz, weights) + [sz.token_spec(sz.width)],
        [sz.sent_spec()] + [sz.token_spec(w) for w in widths],
        [jax.ShapeDtypeStruct(sz.sent_shape(), BF16)]
        + [jax.ShapeDtypeStruct((sz.tokens, w), BF16) for w in widths],
        cost(8 * sz.tokens * sz.width * sz.width, 30 * sz.tokens * sz.width),
        "turn",
        x,
        b1,
        fourth,
        gain_one,
        gain_two,
        *weights,
        g,
    )


def weights_kernel(factor, share, n1, dgate, n2, dup, dact, hs, g, out_ref):
    wide = n1.shape[1]
    units = dup.shape[1]
    out_ref[:, :wide] = (t_dot(n1[...], dgate[...]) * factor).astype(BF16)
    out_ref[:, wide : wide + units] = (t_dot(n2[...], dup[...]) * factor).astype(BF16)
    out_ref[:, wide + units : wide + 2 * units] = (t_dot(n2[...], dact[...]) * factor).astype(BF16)
    down = (t_dot(hs[...], g[...]) * factor).astype(BF16)
    ratio = units // wide
    for k in range(units // share):
        at = wide + 2 * units + (k % ratio) * wide
        out_ref[(k // ratio) * share : (k // ratio + 1) * share, at : at + wide] = down[
            k * share : (k + 1) * share, :
        ]


def weight_parts(sz, factor, n1, dgate, n2, dup, dact, hs, g):
    wide = sz.width // NB
    units = dup.shape[1] // NB
    total = wide + 3 * units
    slim = pl.BlockSpec((sz.tokens, wide), lambda i: (0, i))
    broad = pl.BlockSpec((sz.tokens, units), lambda i: (0, i))
    return (
        functools.partial(weights_kernel, factor, sz.width // sz.n),
        NB,
        [slim, slim, slim, broad, broad, broad, slim],
        [pl.BlockSpec((wide, total), lambda i: (i, 0))],
        [jax.ShapeDtypeStruct((sz.width, total), BF16)],
        cost(2 * sz.tokens * sz.width * total, 24 * sz.tokens * sz.width),
        "weight_grads",
        n1,
        dgate,
        n2,
        dup,
        dact,
        hs,
        g,
    )


def last_kernel(sz, x_ref, d_ref, first_ref, gain_ref, mix_ref, dgate_ref, dy_ref, out_ref):
    wide = sz.width // NB
    gain = gain_ref[...]
    for r in range(sz.per):
        at = pl.ds(r * sz.line, sz.line)
        gated = jnp.concatenate(
            [
                dot_t(
                    dgate_ref[at, b * wide : (b + 1) * wide], mix_ref[b * wide : (b + 1) * wide, :]
                )
                for b in range(NB)
            ],
            axis=1,
        )
        d_normed = t_dot(first_ref[r], sz.get(d_ref, r)) + gated
        x = x_ref[at, :].astype(F32)
        out_ref[at, :] = (
            dy_ref[at, :].astype(F32) + norm_back(x, rms_scale(x), gain, d_normed)
        ).astype(BF16)


def last(sz, part, x, d, first, gain, mix, dgate, dy):
    steps = sz.rows // sz.per
    skip = part * steps
    tokens = sz.token_spec(sz.width, skip)
    return call(
        functools.partial(last_kernel, sz),
        steps,
        [
            tokens,
            sz.sent_spec(),
            sz.factor_spec(skip),
            whole((1, sz.width)),
            whole(mix.shape),
            tokens,
            tokens,
        ],
        sz.token_spec(sz.width),
        jax.ShapeDtypeStruct((sz.tokens, sz.width), BF16),
        cost(2 * sz.tokens * sz.width * 384, 10 * sz.tokens * sz.width),
        "last",
        x,
        d,
        first,
        gain,
        mix,
        dgate,
        dy,
    )


def shift(array, by):
    length = lax.axis_size("section")
    pairs = [(i, i + by) for i in range(length) if 0 <= i + by < length]
    return lax.ppermute(array, "section", pairs)


def shards(
    section_input,
    stashed_input,
    output_grad,
    gain_mixer,
    gain_channel,
    factor_first,
    factor_second,
    spectrum,
    factor_third,
    factor_fourth,
    mixer_gate,
    channel_up,
    channel_gate,
    channel_down,
):
    first = factor_first[0]
    fourth = factor_fourth[0]
    n = lax.axis_size("seq")
    rows = first.shape[0]
    cols = factor_second.shape[1]
    width = section_input.shape[2]
    sz = Sizes(n, rows, cols, width)
    size = sz.tall * cols
    kernel_here = spectrum[0].reshape(size, width)
    mix, up, act, down = mixer_gate[0], channel_up[0], channel_gate[0], channel_down[0]
    gain_one, gain_two = gain_mixer, gain_channel
    xa, xb, g = section_input[0], stashed_input[0], output_grad[0]
    factor = 1.0 / math.sqrt(sz.tall * sz.line)

    everything = (0, rows)
    weights = (mix, up, act, down)
    wide = expand(sz, factor_second[0], factor_third[0])
    (sent_b,) = call(*front_parts(sz, xb, gain_one, first))
    recv_b, sent_a = call_exchanging(
        sz, sz.to_send(sent_b), everything, 1, *front_parts(sz, xa, gain_one, first)
    )
    recv_a, out_b, mixed_b = call_exchanging(
        sz,
        sz.to_send(sent_a),
        everything,
        2,
        *middle_parts(sz, sz.to_flat(recv_b), wide, kernel_here, True),
    )
    rows_b, out_a = call_exchanging(
        sz,
        sz.from_flat(out_b),
        everything,
        3,
        *middle_parts(sz, sz.to_flat(recv_a), wide, kernel_here, False),
    )
    rows_a, sent, dy, dgate, n1, n2, hs, dup, dact = call_exchanging(
        sz,
        sz.from_flat(out_a),
        everything,
        4,
        *turn_parts(sz, xb, sz.to_rows(rows_b), fourth, gain_one, gain_two, *weights, g),
    )
    d_cols, out = call_exchanging(
        sz,
        sz.to_send(sent),
        everything,
        5,
        *tail_parts(sz, xa, sz.to_rows(rows_a), fourth, gain_one, gain_two, *weights),
    )
    next_input = shift(out, 1)
    d_out, spectrum_grad = middle_back(sz, sz.to_flat(d_cols), wide, kernel_here, mixed_b)
    d_out = sz.from_flat(d_out)
    halves = 2 if rows % 2 == 0 else 1
    half = rows // halves
    sh = Sizes(n, half, cols, width)
    d_rows, grads = call_exchanging(
        sz, d_out, (0, half), 6, *weight_parts(sz, factor, n1, dgate, n2, dup, dact, hs, g)
    )
    upstream = []
    for part in range(halves):
        if part:
            (d_rows,) = call_exchanging(
                sz, d_out, (part * half, half), 6 + part, lambda: None, 1, [], [], [], cost(0, 0), "rest"
            )
        dx = last(sh, part, xb, sh.to_rows(d_rows), first, gain_one, mix, dgate, dy)
        upstream.append(shift(dx, -1))
    upstream = jnp.concatenate(upstream, axis=0)
    grads = lax.psum_scatter(grads, "seq", scatter_dimension=0, tiled=True)
    w, u = width // NB, up.shape[1]
    down_grad = jnp.concatenate(
        [grads[:, w + 2 * u + k * w : w + 2 * u + (k + 1) * w] for k in range(u // w)], axis=0
    )
    return (
        next_input[None],
        upstream[None],
        spectrum_grad.reshape(spectrum.shape),
        grads[None, :, :w],
        grads[None, :, w : w + u],
        grads[None, :, w + u : w + 2 * u],
        down_grad[None],
    )


def solution(mesh):
    in_specs = (
        P("section", "seq", None),
        P("section", "seq", None),
        P("section", "seq", None),
        P("section", None),
        P("section", None),
        P("section", "seq", None, None),
        P("section", "seq", None, None),
        P("section", None, "seq", None),
        P("section", "seq", None, None),
        P("section", "seq", None, None),
        P("section", None, None),
        P("section", None, None),
        P("section", None, None),
        P("section", None, None),
    )
    out_specs = (
        P("section", "seq", None),
        P("section", "seq", None),
        P("section", None, "seq", None),
        P("section", "seq", None),
        P("section", "seq", None),
        P("section", "seq", None),
        P("section", "seq", None),
    )
    return jax.shard_map(shards, mesh=mesh, in_specs=in_specs, out_specs=out_specs, check_vma=False)
```

```python
import functools
import math

import jax
import jax.numpy as jnp
from jax import lax
from jax.experimental import pallas as pl
from jax.experimental.pallas import tpu as pltpu
from jax.sharding import PartitionSpec as P

NB = 4
EPS = 1e-06
F32 = jnp.float32
BF16 = jnp.bfloat16
VMEM = 56 * 1024 * 1024


def dot(a, b):
    return jnp.dot(a, b, preferred_element_type=F32)


def dot_t(a, b):
    return lax.dot_general(a, b, (((1,), (1,)), ((), ())), preferred_element_type=F32)


def t_dot(a, b):
    return lax.dot_general(a, b, (((0,), (0,)), ((), ())), preferred_element_type=F32)


def rms_scale(v):
    return lax.rsqrt(jnp.mean(v * v, axis=-1, keepdims=True) + EPS)


def norm_back(v, scale, gain, grad):
    scaled = gain * grad
    return scale * scaled - v * (scale * scale * scale) * jnp.mean(
        scaled * v, axis=-1, keepdims=True
    )


def cols_of(array, b, width):
    return array[:, b * width : (b + 1) * width]


def call(body, grid, in_specs, out_specs, out_shape, price, name, *args):
    return pl.pallas_call(
        body,
        grid=(grid,),
        in_specs=in_specs,
        out_specs=out_specs,
        out_shape=out_shape,
        compiler_params=pltpu.CompilerParams(
            dimension_semantics=("arbitrary",), vmem_limit_bytes=VMEM
        ),
        cost_estimate=price,
        name=name,
    )(*args)


def exchange(n, source, target, send_sem, recv_sem, own_sem):
    me = lax.axis_index("seq")
    chips = n // 2 if n % 2 == 0 else n
    cores = n // chips
    chip, core = me // cores, lax.rem(me, cores)

    def other(r):
        if chips == 4:
            return (chip, chip + 1 - 2 * lax.rem(chip, 2), lax.rem(chip + 2, 4), 3 - chip)[r]
        return lax.rem(chip + r, chips)

    def copy_to(far_chip, relation, c):
        peer = far_chip * cores + lax.rem(core + c, cores)
        index = relation * cores + c - 1
        return pltpu.make_async_remote_copy(
            src_ref=source(peer),
            dst_ref=target,
            send_sem=send_sem(index),
            recv_sem=recv_sem(index),
            device_id={"seq": peer},
            device_id_type=pl.DeviceIdType.MESH,
        )

    def own_copy():
        return pltpu.make_async_copy(
            source(me), target, own_sem
        )

    def start_all():
        relations = [(other(r), r) for r in range(1, chips)]
        if chips == 4 and cores == 2:
            one, two = relations[0][0], relations[1][0]
            relations[0] = (one + core * (two - one), 1 + core)
            relations[1] = (two + core * (one - two), 2 - core)
        for far_chip, r in relations:
            for c in range(cores):
                copy_to(far_chip, r, c).start()
        for c in range(1, cores):
            copy_to(chip, 0, c).start()
        own_copy().start()

    def wait_all():
        own_copy().wait()
        for r in range(chips):
            for c in range(cores):
                if r or c:
                    copy_to(other(r), r, c).wait()

    return start_all, wait_all


def greet(n, others=()):
    barrier = pltpu.get_barrier_semaphore()
    me = lax.axis_index("seq")
    devices = [{"seq": lax.rem(me + k, n)} for k in range(1, n)] + list(others)
    for device in devices:
        pl.semaphore_signal(
            barrier, inc=1, device_id=device, device_id_type=pl.DeviceIdType.MESH
        )
    pl.semaphore_wait(barrier, len(devices))


def call_exchanging(
    sz, send, span, cid, body, grid, in_specs, out_specs, out_shape, price, name, *args
):
    n = sz.n
    count = len(in_specs)

    def kernel(send_ref, *refs):
        ins, recv_ref = refs[:count], refs[count]
        outs = refs[count + 1 : -3]
        send_sem, recv_sem, own_sem = refs[-3:]
        step = pl.program_id(0)
        me = lax.axis_index("seq")

        start_all, wait_all = exchange(
            n,
            lambda peer: send_ref.at[peer, pl.ds(span[0], span[1])],
            recv_ref.at[me],
            lambda k: send_sem.at[k],
            lambda k: recv_sem.at[k],
            own_sem,
        )

        @pl.when(step == 0)
        def _():
            greet(n)
            start_all()

        body(*ins, *outs)

        @pl.when(step == grid - 1)
        def _():
            wait_all()

    shape = (n, span[1]) + send.shape[2:]
    return pl.pallas_call(
        kernel,
        grid=(grid,),
        in_specs=[pl.BlockSpec(memory_space=pl.ANY)] + in_specs,
        out_specs=[pl.BlockSpec(memory_space=pl.ANY)] + out_specs,
        out_shape=[jax.ShapeDtypeStruct(shape, send.dtype)] + out_shape,
        scratch_shapes=[
            pltpu.SemaphoreType.DMA((n - 1,)),
            pltpu.SemaphoreType.DMA((n - 1,)),
            pltpu.SemaphoreType.DMA(()),
        ],
        compiler_params=pltpu.CompilerParams(
            dimension_semantics=("arbitrary",),
            vmem_limit_bytes=VMEM,
            collective_id=cid,
            has_side_effects=True,
        ),
        cost_estimate=price,
        name=name,
    )(send, *args)


def cost(flops, nbytes):
    return pl.CostEstimate(flops=int(flops), bytes_accessed=int(nbytes), transcendentals=0)


class Sizes:
    def __init__(self, n, rows, cols, width):
        self.n = n
        self.rows = rows
        self.cols = cols
        self.width = width
        self.line = n * cols
        self.tall = n * rows
        self.tokens = rows * self.line
        self.per = 2 if rows % 2 == 0 else 1
        self.aligned = cols % 16 == 0
        self.groups = cols // 8 if cols % 8 == 0 else 1

    def sent_shape(self):
        if self.aligned:
            return (self.n, self.rows, self.cols, self.width)
        return (self.rows, self.line, self.width)

    def sent_spec(self):
        if self.aligned:
            return pl.BlockSpec(
                (self.n, self.per, self.cols, self.width), lambda i: (0, i, 0, 0)
            )
        return pl.BlockSpec((self.per, self.line, self.width), lambda i: (i, 0, 0))

    def put(self, ref, r, value):
        if self.aligned:
            ref[:, r] = value.reshape(self.n, self.cols, self.width)
        else:
            ref[r] = value

    def get(self, ref, r):
        if self.aligned:
            return ref[:, r].reshape(self.line, self.width)
        return ref[r]

    def to_send(self, array):
        if self.aligned:
            return array
        return array.reshape(self.rows, self.n, self.cols, self.width).transpose(1, 0, 2, 3)

    def to_flat(self, array):
        return array.reshape(self.tall * self.cols, self.width)

    def from_flat(self, array):
        return array.reshape(self.n, self.rows, self.cols, self.width)

    def to_rows(self, array):
        if self.aligned:
            return array
        return array.transpose(1, 0, 2, 3).reshape(-1, self.line, self.width)

    def token_spec(self, width, skip=0):
        return pl.BlockSpec((self.per * self.line, width), lambda i: (i + skip, 0))

    def factor_spec(self, skip=0):
        return pl.BlockSpec((self.per, self.line, self.line), lambda i: (i + skip, 0, 0))


def whole(shape):
    return pl.BlockSpec(shape, lambda i: (0,) * len(shape))


def front_kernel(sz, x_ref, gain_ref, first_ref, sent_ref):
    for r in range(sz.per):
        x = x_ref[pl.ds(r * sz.line, sz.line), :].astype(F32)
        normed = (x * rms_scale(x) * gain_ref[...]).astype(BF16)
        sz.put(sent_ref, r, dot(first_ref[r], normed).astype(BF16))


def front_parts(sz, x, gain, first):
    return (
        functools.partial(front_kernel, sz),
        sz.rows // sz.per,
        [sz.token_spec(sz.width), whole((1, sz.width)), sz.factor_spec()],
        [sz.sent_spec()],
        [jax.ShapeDtypeStruct(sz.sent_shape(), BF16)],
        cost(2 * sz.tokens * sz.line * sz.width, 4 * sz.tokens * sz.width),
        "front",
        x,
        gain,
        first,
    )


def expand_piece(factor, cols, tall):
    size = tall * cols

    def index(axis):
        return lax.broadcasted_iota(jnp.int32, (size, size), axis)

    swap = (index(0) // cols == index(1) % tall) & (index(0) % cols == index(1) // tall)
    swap = swap.astype(F32).astype(BF16)
    thin = dot(swap, factor.reshape(size, tall)).astype(BF16)
    pick = lax.broadcasted_iota(jnp.int32, (tall, size), 1) // cols
    pick = (pick == lax.broadcasted_iota(jnp.int32, (tall, size), 0)).astype(F32).astype(BF16)
    return jnp.where(index(0) % cols == index(1) % cols, dot(thin, pick), 0.0)


def front_expand_kernel(sz, steps, x_ref, gain_ref, first_ref, second, third, sent_ref, wide_ref):
    front_kernel(sz, x_ref, gain_ref, first_ref, sent_ref)
    inner = sz.cols // sz.groups
    step = pl.program_id(0)
    for k in range(2 * sz.groups):

        @pl.when(step == k % steps)
        def _():
            which, g = k // sz.groups, k % sz.groups
            factor = (second, third)[which][g * inner : (g + 1) * inner]
            piece = expand_piece(factor, inner, sz.tall)
            wide_ref[which, g] = piece.astype(BF16)
            wide_ref[3 - which, g] = piece.T.astype(BF16)


def front_expand_parts(sz, x, gain, first, second, third):
    body, grid, ins, outs, shapes, price, name, *args = front_parts(sz, x, gain, first)
    size = sz.tall * sz.cols // sz.groups
    wide = (4, sz.groups, size, size)
    return (
        functools.partial(front_expand_kernel, sz, grid),
        grid,
        ins + [whole(second.shape), whole(third.shape)],
        outs + [whole(wide)],
        shapes + [jax.ShapeDtypeStruct(wide, BF16)],
        price,
        name,
        *args,
        second,
        third,
    )


def mix_rows(sz, wide_ref, x):
    if sz.groups == 1:
        return dot(wide_ref[0, 0], x.astype(BF16))
    part = x.shape[1]
    inner = sz.cols // sz.groups
    x = x.reshape(sz.tall, sz.cols, part)
    outs = []
    for g in range(sz.groups):
        piece = x[:, g * inner : (g + 1) * inner].reshape(sz.tall * inner, part).astype(BF16)
        outs.append(dot(wide_ref[0, g], piece).reshape(sz.tall, inner, part))
    return jnp.concatenate(outs, axis=1).reshape(sz.tall * sz.cols, part)


def middle_kernel(sz, x_ref, second_ref, third_ref, spectrum_ref, out_ref, *mixed_ref):
    mixed = mix_rows(sz, second_ref, x_ref[...].astype(F32))
    if mixed_ref:
        mixed_ref[0][...] = mixed
    filtered = mixed * spectrum_ref[...].astype(F32)
    out_ref[...] = mix_rows(sz, third_ref, filtered).astype(BF16)


def wide_spec(wide, which):
    return pl.BlockSpec((1,) + wide.shape[1:], lambda i: (which, 0, 0, 0))


def middle_parts(sz, x, wide, spectrum, keep):
    size = sz.tall * sz.cols
    part = 256
    strip = pl.BlockSpec((size, part), lambda i: (0, i))
    shapes = [jax.ShapeDtypeStruct((size, sz.width), BF16)]
    if keep:
        shapes.append(jax.ShapeDtypeStruct((size, sz.width), F32))
    return (
        functools.partial(middle_kernel, sz),
        sz.width // part,
        [strip, wide_spec(wide, 0), wide_spec(wide, 1), strip],
        [strip] * len(shapes),
        shapes,
        cost(4 * size * size * sz.width // sz.groups, 10 * size * sz.width),
        "middle",
        x,
        wide,
        wide,
        spectrum,
    )


def middle_back_kernel(
    sz, d_ref, third_ref, second_ref, spectrum_ref, mixed_ref, out_ref, grad_ref
):
    d_filtered = mix_rows(sz, third_ref, d_ref[...].astype(F32))
    grad_ref[...] = (d_filtered * mixed_ref[...]).astype(BF16)
    d_mixed = d_filtered * spectrum_ref[...].astype(F32)
    out_ref[...] = mix_rows(sz, second_ref, d_mixed).astype(BF16)


def middle_back(sz, d, wide, spectrum, mixed):
    size = sz.tall * sz.cols
    part = 256
    strip = pl.BlockSpec((size, part), lambda i: (0, i))
    return call(
        functools.partial(middle_back_kernel, sz),
        sz.width // part,
        [strip, wide_spec(wide, 2), wide_spec(wide, 3), strip, strip],
        [strip, strip],
        [jax.ShapeDtypeStruct((size, sz.width), BF16)] * 2,
        cost(4 * size * size * sz.width // sz.groups, 12 * size * sz.width),
        "middle_back",
        d,
        wide,
        wide,
        spectrum,
        mixed,
    )


def tail_front(sz, x_ref, b1_ref, fourth_ref, gain_one, mix_ref):
    x = x_ref[...].astype(F32)
    normed = (x * rms_scale(x) * gain_one).astype(BF16)
    collected = [dot(fourth_ref[r], sz.get(b1_ref, r)) for r in range(sz.per)]
    back = collected[0] if sz.per == 1 else jnp.concatenate(collected, axis=0)
    wide = sz.width // NB
    gate = jnp.concatenate(
        [
            dot(cols_of(normed, b, wide), mix_ref[b * wide : (b + 1) * wide, :])
            for b in range(NB)
        ],
        axis=1,
    )
    y1 = (x + back * gate).astype(BF16)
    return normed, back, gate, y1


def tail_kernel(
    sz,
    x_ref,
    b1_ref,
    fourth_ref,
    gain_one_ref,
    gain_two_ref,
    mix_ref,
    up_ref,
    act_ref,
    down_ref,
    out_ref,
):
    _, _, _, y1 = tail_front(sz, x_ref, b1_ref, fourth_ref, gain_one_ref[...], mix_ref)
    y = y1.astype(F32)
    n2 = (y * rms_scale(y) * gain_two_ref[...]).astype(BF16)
    wide = sz.width // NB
    hidden = []
    for b in range(NB):
        rows = slice(b * wide, (b + 1) * wide)
        lifted = dot(n2[:, rows], up_ref[rows, :])
        gated = dot(n2[:, rows], act_ref[rows, :])
        hidden.append((gated * jax.nn.sigmoid(gated) * lifted).astype(BF16))
    units = hidden[0].shape[1]
    piece = units // NB
    for b in range(NB):
        mixed = jnp.concatenate([cols_of(h, b, piece) for h in hidden], axis=1)
        out_ref[:, b * wide : (b + 1) * wide] = (
            cols_of(y, b, wide) + dot(mixed, down_ref[b * units : (b + 1) * units, :])
        ).astype(BF16)


def tail_specs(sz, weights):
    return [
        sz.token_spec(sz.width),
        sz.sent_spec(),
        sz.factor_spec(),
        whole((1, sz.width)),
        whole((1, sz.width)),
    ] + [whole(w.shape) for w in weights]


def tail_parts(sz, x, b1, fourth, gain_one, gain_two, *weights):
    return (
        functools.partial(tail_kernel, sz),
        sz.rows // sz.per,
        tail_specs(sz, weights),
        [sz.token_spec(sz.width)],
        [jax.ShapeDtypeStruct((sz.tokens, sz.width), BF16)],
        cost(4 * sz.tokens * sz.width * sz.width, 8 * sz.tokens * sz.width),
        "tail",
        x,
        b1,
        fourth,
        gain_one,
        gain_two,
        *weights,
    )


def turn_kernel(
    sz,
    x_ref,
    b1_ref,
    fourth_ref,
    gain_one_ref,
    gain_two_ref,
    mix_ref,
    up_ref,
    act_ref,
    down_ref,
    g_ref,
    sent_ref,
    dy_ref,
    dgate_ref,
    n1_ref,
    n2_ref,
    hs_ref,
    dup_ref,
    dact_ref,
):
    n1, back, gate, y1 = tail_front(sz, x_ref, b1_ref, fourth_ref, gain_one_ref[...], mix_ref)
    n1_ref[...] = n1
    y = y1.astype(F32)
    scale_two = rms_scale(y)
    n2 = (y * scale_two * gain_two_ref[...]).astype(BF16)
    n2_ref[...] = n2
    wide = sz.width // NB
    units = up_ref.shape[1]
    piece = units // NB
    d_shuffled = [
        dot_t(g_ref[:, b * wide : (b + 1) * wide], down_ref[b * units : (b + 1) * units, :]).astype(
            BF16
        )
        for b in range(NB)
    ]
    d_n2 = []
    for b in range(NB):
        rows = slice(b * wide, (b + 1) * wide)
        lifted = dot(n2[:, rows], up_ref[rows, :])
        gated = dot(n2[:, rows], act_ref[rows, :])
        sigma = jax.nn.sigmoid(gated)
        silu = gated * sigma
        hidden = (silu * lifted).astype(BF16)
        for k in range(NB):
            at = k * units + b * piece
            hs_ref[:, at : at + piece] = cols_of(hidden, k, piece)
        d_hidden = jnp.concatenate([cols_of(d, b, piece) for d in d_shuffled], axis=1).astype(F32)
        d_lift = (d_hidden * silu).astype(BF16)
        d_gated = (d_hidden * lifted * sigma * (1.0 + gated * (1.0 - sigma))).astype(BF16)
        dup_ref[:, b * units : (b + 1) * units] = d_lift
        dact_ref[:, b * units : (b + 1) * units] = d_gated
        d_n2.append(dot_t(d_lift, up_ref[rows, :]) + dot_t(d_gated, act_ref[rows, :]))
    d_n2 = jnp.concatenate(d_n2, axis=1)
    dy = (g_ref[...].astype(F32) + norm_back(y, scale_two, gain_two_ref[...], d_n2)).astype(BF16)
    dy_ref[...] = dy
    dyw = dy.astype(F32)
    dgate_ref[...] = (dyw * back).astype(BF16)
    d_back = (dyw * gate).astype(BF16)
    for r in range(sz.per):
        part = d_back[r * sz.line : (r + 1) * sz.line, :]
        sz.put(sent_ref, r, t_dot(fourth_ref[r], part).astype(BF16))


def turn_parts(sz, x, b1, fourth, gain_one, gain_two, mix, up, act, down, g):
    weights = (mix, up, act, down)
    units = NB * up.shape[1]
    widths = [sz.width] * 4 + [units] * 3
    return (
        functools.partial(turn_kernel, sz),
        sz.rows // sz.per,
        tail_specs(sz, weights) + [sz.token_spec(sz.width)],
        [sz.sent_spec()] + [sz.token_spec(w) for w in widths],
        [jax.ShapeDtypeStruct(sz.sent_shape(), BF16)]
        + [jax.ShapeDtypeStruct((sz.tokens, w), BF16) for w in widths],
        cost(8 * sz.tokens * sz.width * sz.width, 30 * sz.tokens * sz.width),
        "turn",
        x,
        b1,
        fourth,
        gain_one,
        gain_two,
        *weights,
        g,
    )


def weights_kernel(factor, share, n1, dgate, n2, dup, dact, hs, g, out_ref):
    wide = n1.shape[1]
    units = dup.shape[1]
    out_ref[:, :wide] = (t_dot(n1[...], dgate[...]) * factor).astype(BF16)
    out_ref[:, wide : wide + units] = (t_dot(n2[...], dup[...]) * factor).astype(BF16)
    out_ref[:, wide + units : wide + 2 * units] = (t_dot(n2[...], dact[...]) * factor).astype(BF16)
    down = (t_dot(hs[...], g[...]) * factor).astype(BF16)
    ratio = units // wide
    for k in range(units // share):
        at = wide + 2 * units + (k % ratio) * wide
        out_ref[(k // ratio) * share : (k // ratio + 1) * share, at : at + wide] = down[
            k * share : (k + 1) * share, :
        ]


def weight_parts(sz, factor, n1, dgate, n2, dup, dact, hs, g):
    wide = sz.width // NB
    units = dup.shape[1] // NB
    total = wide + 3 * units
    slim = pl.BlockSpec((sz.tokens, wide), lambda i: (0, i))
    broad = pl.BlockSpec((sz.tokens, units), lambda i: (0, i))
    return (
        functools.partial(weights_kernel, factor, sz.width // sz.n),
        NB,
        [slim, slim, slim, broad, broad, broad, slim],
        [pl.BlockSpec((wide, total), lambda i: (i, 0))],
        [jax.ShapeDtypeStruct((sz.width, total), BF16)],
        cost(2 * sz.tokens * sz.width * total, 24 * sz.tokens * sz.width),
        "weight_grads",
        n1,
        dgate,
        n2,
        dup,
        dact,
        hs,
        g,
    )


def last_kernel(sz, x_ref, d_ref, first_ref, gain_ref, mix_ref, dgate_ref, dy_ref, out_ref):
    wide = sz.width // NB
    gain = gain_ref[...]
    for r in range(sz.per):
        at = pl.ds(r * sz.line, sz.line)
        gated = jnp.concatenate(
            [
                dot_t(
                    dgate_ref[at, b * wide : (b + 1) * wide], mix_ref[b * wide : (b + 1) * wide, :]
                )
                for b in range(NB)
            ],
            axis=1,
        )
        d_normed = t_dot(first_ref[r], sz.get(d_ref, r)) + gated
        x = x_ref[at, :].astype(F32)
        out_ref[at, :] = (
            dy_ref[at, :].astype(F32) + norm_back(x, rms_scale(x), gain, d_normed)
        ).astype(BF16)


def last(sz, part, x, d, first, gain, mix, dgate, dy):
    steps = sz.rows // sz.per
    skip = part * steps
    tokens = sz.token_spec(sz.width, skip)
    return call(
        functools.partial(last_kernel, sz),
        steps,
        [
            tokens,
            sz.sent_spec(),
            sz.factor_spec(skip),
            whole((1, sz.width)),
            whole(mix.shape),
            tokens,
            tokens,
        ],
        sz.token_spec(sz.width),
        jax.ShapeDtypeStruct((sz.tokens, sz.width), BF16),
        cost(2 * sz.tokens * sz.width * 384, 10 * sz.tokens * sz.width),
        "last",
        x,
        d,
        first,
        gain,
        mix,
        dgate,
        dy,
    )


def join(one, two):
    a, b = len(one[2]), len(two[2])
    c = len(one[3])

    def body(*refs):
        ins, outs = refs[: a + b], refs[a + b :]
        one[0](*ins[:a], *outs[:c])
        two[0](*ins[a:], *outs[c:])

    return (
        (body, one[1], one[2] + two[2], one[3] + two[3], one[4] + two[4], one[5], one[6])
        + tuple(one[7:])
        + tuple(two[7:])
    )


def finish_kernel(
    sz,
    parts,
    send_ref,
    x_ref,
    first_ref,
    gain_ref,
    mix_ref,
    dgate_ref,
    dy_ref,
    out_ref,
    recv,
    dx,
    zero,
    send_sem,
    recv_sem,
    own_sem,
    up_send,
    up_recv,
    zero_sem,
):
    step = pl.program_id(0)
    me, section = lax.axis_index("seq"), lax.axis_index("section")
    sections = lax.axis_size("section")
    some = sz.rows // parts
    wide = sz.width // NB

    def part_exchange(p):
        return exchange(
            sz.n,
            lambda peer: send_ref.at[peer, pl.ds(p * some, some)],
            recv.at[p, me],
            lambda k: send_sem.at[p, k],
            lambda k: recv_sem.at[p, k],
            own_sem.at[p],
        )

    def up_copy(p):
        return pltpu.make_async_remote_copy(
            src_ref=dx.at[p],
            dst_ref=out_ref.at[p],
            send_sem=up_send.at[p],
            recv_sem=up_recv.at[p],
            device_id={"section": lax.rem(section + sections - 1, sections)},
            device_id_type=pl.DeviceIdType.MESH,
        )

    def zero_copy(p):
        return pltpu.make_async_copy(zero, out_ref.at[p], zero_sem.at[p])

    top = section == sections - 1

    @pl.when(step == 0)
    def _():
        greet(
            sz.n,
            [
                {"section": lax.rem(section + 1, sections)},
                {"section": lax.rem(section + sections - 1, sections)},
            ],
        )
        for p in range(parts):
            part_exchange(p)[0]()

        @pl.when(top)
        def _():
            zero[...] = jnp.zeros_like(zero)
            for p in range(parts):
                zero_copy(p).start()

    gain = gain_ref[...]
    gated, scales = [], []
    for r in range(some):
        at = pl.ds(r * sz.line, sz.line)
        gated.append(
            jnp.concatenate(
                [
                    dot_t(
                        dgate_ref[at, b * wide : (b + 1) * wide],
                        mix_ref[b * wide : (b + 1) * wide, :],
                    )
                    for b in range(NB)
                ],
                axis=1,
            )
        )
        scales.append(rms_scale(x_ref[at, :].astype(F32)))
    part_exchange(step)[1]()
    for r in range(some):
        at = pl.ds(r * sz.line, sz.line)
        d = recv[step, :, r].reshape(sz.line, sz.width)
        d_normed = t_dot(first_ref[r], d) + gated[r]
        x = x_ref[at, :].astype(F32)
        dx[step, at, :] = (
            dy_ref[at, :].astype(F32) + norm_back(x, scales[r], gain, d_normed)
        ).astype(BF16)

    @pl.when(section > 0)
    def _():
        up_copy(step).start()

    @pl.when(step == parts - 1)
    def _():
        @pl.when(section > 0)
        def _():
            for p in range(parts):
                up_copy(p).wait_send()

        @pl.when(section < sections - 1)
        def _():
            for p in range(parts):
                up_copy(p).wait_recv()

        @pl.when(top)
        def _():
            for p in range(parts):
                zero_copy(p).wait()


def finish(sz, parts, cid, d, x, first, gain, mix, dgate, dy):
    some = sz.rows // parts
    tokens = some * sz.line
    strip = pl.BlockSpec((tokens, sz.width), lambda i: (i, 0))
    out = pl.pallas_call(
        functools.partial(finish_kernel, sz, parts),
        grid=(parts,),
        in_specs=[
            pl.BlockSpec(memory_space=pl.ANY),
            strip,
            pl.BlockSpec((some, sz.line, sz.line), lambda i: (i, 0, 0)),
            whole((1, sz.width)),
            whole(mix.shape),
            strip,
            strip,
        ],
        out_specs=pl.BlockSpec(memory_space=pl.ANY),
        out_shape=jax.ShapeDtypeStruct((parts, tokens, sz.width), BF16),
        scratch_shapes=[
            pltpu.VMEM((parts, sz.n, some, sz.cols, sz.width), BF16),
            pltpu.VMEM((parts, tokens, sz.width), BF16),
            pltpu.VMEM((tokens, sz.width), BF16),
            pltpu.SemaphoreType.DMA((parts, sz.n - 1)),
            pltpu.SemaphoreType.DMA((parts, sz.n - 1)),
            pltpu.SemaphoreType.DMA((parts,)),
            pltpu.SemaphoreType.DMA((parts,)),
            pltpu.SemaphoreType.DMA((parts,)),
            pltpu.SemaphoreType.DMA((parts,)),
        ],
        compiler_params=pltpu.CompilerParams(
            dimension_semantics=("arbitrary",),
            vmem_limit_bytes=VMEM,
            collective_id=cid,
            has_side_effects=True,
        ),
        cost_estimate=cost(2 * sz.tokens * sz.width * 384, 10 * sz.tokens * sz.width),
        name="finish",
    )(d, x, first, gain, mix, dgate, dy)
    return out.reshape(sz.tokens, sz.width)


def split_kernel(wide, units, total, mix_ref, up_ref, act_ref, down_ref):
    mix_ref[...] = total[:, :wide]
    up_ref[...] = total[:, wide : wide + units]
    act_ref[...] = total[:, wide + units : wide + 2 * units]
    share = total.shape[0]
    for k in range(units // wide):
        at = wide + 2 * units + k * wide
        down_ref[k * share : (k + 1) * share, :] = total[:, at : at + wide]


def split_grads(total, wide, units):
    share = total.shape[0]
    shapes = [(share, wide), (share, units), (share, units), (share * units // wide, wide)]
    return call(
        functools.partial(split_kernel, wide, units),
        1,
        [whole(total.shape)],
        [whole(shape) for shape in shapes],
        [jax.ShapeDtypeStruct(shape, BF16) for shape in shapes],
        cost(0, 4 * share * (wide + 3 * units)),
        "split_grads",
        total,
    )


def shift(array, by):
    length = lax.axis_size("section")
    pairs = [(i, i + by) for i in range(length) if 0 <= i + by < length]
    return lax.ppermute(array, "section", pairs)


def shards(
    section_input,
    stashed_input,
    output_grad,
    gain_mixer,
    gain_channel,
    factor_first,
    factor_second,
    spectrum,
    factor_third,
    factor_fourth,
    mixer_gate,
    channel_up,
    channel_gate,
    channel_down,
):
    first = factor_first[0]
    fourth = factor_fourth[0]
    n = lax.axis_size("seq")
    rows = first.shape[0]
    cols = factor_second.shape[1]
    width = section_input.shape[2]
    sz = Sizes(n, rows, cols, width)
    size = sz.tall * cols
    kernel_here = spectrum[0].reshape(size, width)
    mix, up, act, down = mixer_gate[0], channel_up[0], channel_gate[0], channel_down[0]
    gain_one, gain_two = gain_mixer, gain_channel
    xa, xb, g = section_input[0], stashed_input[0], output_grad[0]
    factor = 1.0 / math.sqrt(sz.tall * sz.line)

    everything = (0, rows)
    weights = (mix, up, act, down)
    (sent_b,) = call(*front_parts(sz, xb, gain_one, first))
    recv_b, sent_a, wide = call_exchanging(
        sz,
        sz.to_send(sent_b),
        everything,
        1,
        *front_expand_parts(sz, xa, gain_one, first, factor_second[0], factor_third[0]),
    )
    recv_a, out_b, mixed_b = call_exchanging(
        sz,
        sz.to_send(sent_a),
        everything,
        2,
        *middle_parts(sz, sz.to_flat(recv_b), wide, kernel_here, True),
    )
    rows_b, out_a = call_exchanging(
        sz,
        sz.from_flat(out_b),
        everything,
        3,
        *middle_parts(sz, sz.to_flat(recv_a), wide, kernel_here, False),
    )
    rows_a, sent, dy, dgate, n1, n2, hs, dup, dact = call_exchanging(
        sz,
        sz.from_flat(out_a),
        everything,
        4,
        *turn_parts(sz, xb, sz.to_rows(rows_b), fourth, gain_one, gain_two, *weights, g),
    )
    work = tail_parts(sz, xa, sz.to_rows(rows_a), fourth, gain_one, gain_two, *weights)
    more = weight_parts(sz, factor, n1, dgate, n2, dup, dact, hs, g)
    if work[1] == more[1]:
        d_cols, out, grads = call_exchanging(
            sz, sz.to_send(sent), everything, 5, *join(work, more)
        )
    else:
        d_cols, out = call_exchanging(sz, sz.to_send(sent), everything, 5, *work)
        (grads,) = call(*more)
    next_input = shift(out, 1)
    d_out, spectrum_grad = middle_back(sz, sz.to_flat(d_cols), wide, kernel_here, mixed_b)
    d_out = sz.from_flat(d_out)
    parts = max(k for k in (1, 2, 4) if rows % k == 0)
    some = rows // parts
    sp = Sizes(n, some, cols, width)
    grads, d_out = lax.optimization_barrier((grads, d_out))
    total = lax.psum_scatter(grads, "seq", scatter_dimension=0, tiled=True)
    if sz.aligned:
        upstream = finish(sz, parts, 6, d_out, xb, first, gain_one, mix, dgate, dy)
    else:
        dx = []
        for part in range(parts):
            work = (lambda: None, 1, [], [], [], cost(0, 0), "rest")
            (d_rows,) = call_exchanging(sz, d_out, (part * some, some), 6 + part, *work)
            dx.append(last(sp, part, xb, sp.to_rows(d_rows), first, gain_one, mix, dgate, dy))
        upstream = shift(jnp.concatenate(dx, axis=0), -1)
    grads = split_grads(total, width // NB, up.shape[1])
    return (
        next_input[None],
        upstream[None],
        spectrum_grad.reshape(spectrum.shape),
    ) + tuple(grad[None] for grad in grads)


def solution(mesh):
    in_specs = (
        P("section", "seq", None),
        P("section", "seq", None),
        P("section", "seq", None),
        P("section", None),
        P("section", None),
        P("section", "seq", None, None),
        P("section", "seq", None, None),
        P("section", None, "seq", None),
        P("section", "seq", None, None),
        P("section", "seq", None, None),
        P("section", None, None),
        P("section", None, None),
        P("section", None, None),
        P("section", None, None),
    )
    out_specs = (
        P("section", "seq", None),
        P("section", "seq", None),
        P("section", None, "seq", None),
        P("section", "seq", None),
        P("section", "seq", None),
        P("section", "seq", None),
        P("section", "seq", None),
    )
    return jax.shard_map(shards, mesh=mesh, in_specs=in_specs, out_specs=out_specs, check_vma=False)
```

```python
import functools
import math

import jax
import jax.numpy as jnp
from jax import lax
from jax.experimental import pallas as pl
from jax.experimental.pallas import tpu as pltpu
from jax.sharding import PartitionSpec as P

NB = 4
EPS = 1e-06
F32 = jnp.float32
BF16 = jnp.bfloat16
VMEM = 56 * 1024 * 1024


def dot(a, b):
    return jnp.dot(a, b, preferred_element_type=F32)


def dot_t(a, b):
    return lax.dot_general(a, b, (((1,), (1,)), ((), ())), preferred_element_type=F32)


def t_dot(a, b):
    return lax.dot_general(a, b, (((0,), (0,)), ((), ())), preferred_element_type=F32)


def rms_scale(v):
    return lax.rsqrt(jnp.mean(v * v, axis=-1, keepdims=True) + EPS)


def norm_back(v, scale, gain, grad):
    scaled = gain * grad
    return scale * scaled - v * (scale * scale * scale) * jnp.mean(
        scaled * v, axis=-1, keepdims=True
    )


def cols_of(array, b, width):
    return array[:, b * width : (b + 1) * width]


def call(body, grid, in_specs, out_specs, out_shape, price, name, *args):
    return pl.pallas_call(
        body,
        grid=(grid,),
        in_specs=in_specs,
        out_specs=out_specs,
        out_shape=out_shape,
        compiler_params=pltpu.CompilerParams(
            dimension_semantics=("arbitrary",), vmem_limit_bytes=VMEM
        ),
        cost_estimate=price,
        name=name,
    )(*args)


def exchange(n, source, target, send_sem, recv_sem, own_sem):
    me = lax.axis_index("seq")
    chips = n // 2 if n % 2 == 0 else n
    cores = n // chips
    chip, core = me // cores, lax.rem(me, cores)

    def other(r):
        if chips == 4:
            return (chip, chip + 1 - 2 * lax.rem(chip, 2), lax.rem(chip + 2, 4), 3 - chip)[r]
        return lax.rem(chip + r, chips)

    def copy_to(far_chip, relation, c):
        peer = far_chip * cores + lax.rem(core + c, cores)
        index = relation * cores + c - 1
        return pltpu.make_async_remote_copy(
            src_ref=source(peer),
            dst_ref=target,
            send_sem=send_sem(index),
            recv_sem=recv_sem(index),
            device_id={"seq": peer},
            device_id_type=pl.DeviceIdType.MESH,
        )

    def own_copy():
        return pltpu.make_async_copy(
            source(me), target, own_sem
        )

    def start_all():
        relations = [(other(r), r) for r in range(1, chips)]
        if chips == 4 and cores == 2:
            one, two = relations[0][0], relations[1][0]
            relations[0] = (one + core * (two - one), 1 + core)
            relations[1] = (two + core * (one - two), 2 - core)
        for far_chip, r in relations:
            for c in range(cores):
                copy_to(far_chip, r, c).start()
        for c in range(1, cores):
            copy_to(chip, 0, c).start()
        own_copy().start()

    def wait_all():
        own_copy().wait()
        for r in range(chips):
            for c in range(cores):
                if r or c:
                    copy_to(other(r), r, c).wait()

    return start_all, wait_all


def greet(n, others=()):
    barrier = pltpu.get_barrier_semaphore()
    me = lax.axis_index("seq")
    devices = [{"seq": lax.rem(me + k, n)} for k in range(1, n)] + list(others)
    for device in devices:
        pl.semaphore_signal(
            barrier, inc=1, device_id=device, device_id_type=pl.DeviceIdType.MESH
        )
    pl.semaphore_wait(barrier, len(devices))


def call_exchanging(
    sz, send, span, cid, body, grid, in_specs, out_specs, out_shape, price, name, *args
):
    n = sz.n
    count = len(in_specs)

    def kernel(send_ref, *refs):
        ins, recv_ref = refs[:count], refs[count]
        outs = refs[count + 1 : -3]
        send_sem, recv_sem, own_sem = refs[-3:]
        step = pl.program_id(0)
        me = lax.axis_index("seq")

        start_all, wait_all = exchange(
            n,
            lambda peer: send_ref.at[peer, pl.ds(span[0], span[1])],
            recv_ref.at[me],
            lambda k: send_sem.at[k],
            lambda k: recv_sem.at[k],
            own_sem,
        )

        @pl.when(step == 0)
        def _():
            greet(n)
            start_all()

        body(*ins, *outs)

        @pl.when(step == grid - 1)
        def _():
            wait_all()

    shape = (n, span[1]) + send.shape[2:]
    return pl.pallas_call(
        kernel,
        grid=(grid,),
        in_specs=[pl.BlockSpec(memory_space=pl.ANY)] + in_specs,
        out_specs=[pl.BlockSpec(memory_space=pl.ANY)] + out_specs,
        out_shape=[jax.ShapeDtypeStruct(shape, send.dtype)] + out_shape,
        scratch_shapes=[
            pltpu.SemaphoreType.DMA((n - 1,)),
            pltpu.SemaphoreType.DMA((n - 1,)),
            pltpu.SemaphoreType.DMA(()),
        ],
        compiler_params=pltpu.CompilerParams(
            dimension_semantics=("arbitrary",),
            vmem_limit_bytes=VMEM,
            collective_id=cid,
            has_side_effects=True,
        ),
        cost_estimate=price,
        name=name,
    )(send, *args)


def cost(flops, nbytes):
    return pl.CostEstimate(flops=int(flops), bytes_accessed=int(nbytes), transcendentals=0)


class Sizes:
    def __init__(self, n, rows, cols, width):
        self.n = n
        self.rows = rows
        self.cols = cols
        self.width = width
        self.line = n * cols
        self.tall = n * rows
        self.tokens = rows * self.line
        self.per = 2 if rows % 2 == 0 else 1
        self.aligned = cols % 16 == 0
        self.groups = cols // 8 if cols % 8 == 0 else 1

    def sent_shape(self):
        if self.aligned:
            return (self.n, self.rows, self.cols, self.width)
        return (self.rows, self.line, self.width)

    def sent_spec(self):
        if self.aligned:
            return pl.BlockSpec(
                (self.n, self.per, self.cols, self.width), lambda i: (0, i, 0, 0)
            )
        return pl.BlockSpec((self.per, self.line, self.width), lambda i: (i, 0, 0))

    def put(self, ref, r, value):
        if self.aligned:
            ref[:, r] = value.reshape(self.n, self.cols, self.width)
        else:
            ref[r] = value

    def get(self, ref, r):
        if self.aligned:
            return ref[:, r].reshape(self.line, self.width)
        return ref[r]

    def to_send(self, array):
        if self.aligned:
            return array
        return array.reshape(self.rows, self.n, self.cols, self.width).transpose(1, 0, 2, 3)

    def to_flat(self, array):
        return array.reshape(self.tall * self.cols, self.width)

    def from_flat(self, array):
        return array.reshape(self.n, self.rows, self.cols, self.width)

    def to_rows(self, array):
        if self.aligned:
            return array
        return array.transpose(1, 0, 2, 3).reshape(-1, self.line, self.width)

    def token_spec(self, width, skip=0):
        return pl.BlockSpec((self.per * self.line, width), lambda i: (i + skip, 0))

    def factor_spec(self, skip=0):
        return pl.BlockSpec((self.per, self.line, self.line), lambda i: (i + skip, 0, 0))


def whole(shape):
    return pl.BlockSpec(shape, lambda i: (0,) * len(shape))


def front_kernel(sz, x_ref, gain_ref, first_ref, sent_ref):
    for r in range(sz.per):
        x = x_ref[pl.ds(r * sz.line, sz.line), :].astype(F32)
        normed = (x * rms_scale(x) * gain_ref[...]).astype(BF16)
        sz.put(sent_ref, r, dot(first_ref[r], normed).astype(BF16))


def front_parts(sz, x, gain, first):
    return (
        functools.partial(front_kernel, sz),
        sz.rows // sz.per,
        [sz.token_spec(sz.width), whole((1, sz.width)), sz.factor_spec()],
        [sz.sent_spec()],
        [jax.ShapeDtypeStruct(sz.sent_shape(), BF16)],
        cost(2 * sz.tokens * sz.line * sz.width, 4 * sz.tokens * sz.width),
        "front",
        x,
        gain,
        first,
    )


def expand_piece(factor, cols, tall):
    size = tall * cols

    def index(axis):
        return lax.broadcasted_iota(jnp.int32, (size, size), axis)

    swap = (index(0) // cols == index(1) % tall) & (index(0) % cols == index(1) // tall)
    swap = swap.astype(F32).astype(BF16)
    thin = dot(swap, factor.reshape(size, tall)).astype(BF16)
    pick = lax.broadcasted_iota(jnp.int32, (tall, size), 1) // cols
    pick = (pick == lax.broadcasted_iota(jnp.int32, (tall, size), 0)).astype(F32).astype(BF16)
    return jnp.where(index(0) % cols == index(1) % cols, dot(thin, pick), 0.0)


def front_expand_kernel(sz, steps, x_ref, gain_ref, first_ref, second, third, sent_ref, wide_ref):
    front_kernel(sz, x_ref, gain_ref, first_ref, sent_ref)
    inner = sz.cols // sz.groups
    step = pl.program_id(0)
    for k in range(2 * sz.groups):

        @pl.when(step == k % steps)
        def _():
            which, g = k // sz.groups, k % sz.groups
            factor = (second, third)[which][g * inner : (g + 1) * inner]
            piece = expand_piece(factor, inner, sz.tall)
            wide_ref[which, g] = piece.astype(BF16)
            wide_ref[3 - which, g] = piece.T.astype(BF16)


def front_expand_parts(sz, x, gain, first, second, third):
    body, grid, ins, outs, shapes, price, name, *args = front_parts(sz, x, gain, first)
    size = sz.tall * sz.cols // sz.groups
    wide = (4, sz.groups, size, size)
    return (
        functools.partial(front_expand_kernel, sz, grid),
        grid,
        ins + [whole(second.shape), whole(third.shape)],
        outs + [whole(wide)],
        shapes + [jax.ShapeDtypeStruct(wide, BF16)],
        price,
        name,
        *args,
        second,
        third,
    )


def mix_rows(sz, wide_ref, x):
    if sz.groups == 1:
        return dot(wide_ref[0, 0], x.astype(BF16))
    part = x.shape[1]
    inner = sz.cols // sz.groups
    x = x.reshape(sz.tall, sz.cols, part)
    outs = []
    for g in range(sz.groups):
        piece = x[:, g * inner : (g + 1) * inner].reshape(sz.tall * inner, part).astype(BF16)
        outs.append(dot(wide_ref[0, g], piece).reshape(sz.tall, inner, part))
    return jnp.concatenate(outs, axis=1).reshape(sz.tall * sz.cols, part)


def middle_kernel(sz, x_ref, second_ref, third_ref, spectrum_ref, out_ref, *mixed_ref):
    mixed = mix_rows(sz, second_ref, x_ref[...].astype(F32))
    if mixed_ref:
        mixed_ref[0][...] = mixed
    filtered = mixed * spectrum_ref[...].astype(F32)
    out_ref[...] = mix_rows(sz, third_ref, filtered).astype(BF16)


def wide_spec(wide, which):
    return pl.BlockSpec((1,) + wide.shape[1:], lambda i: (which, 0, 0, 0))


def middle_parts(sz, x, wide, spectrum, keep):
    size = sz.tall * sz.cols
    part = 256
    strip = pl.BlockSpec((size, part), lambda i: (0, i))
    shapes = [jax.ShapeDtypeStruct((size, sz.width), BF16)]
    if keep:
        shapes.append(jax.ShapeDtypeStruct((size, sz.width), F32))
    return (
        functools.partial(middle_kernel, sz),
        sz.width // part,
        [strip, wide_spec(wide, 0), wide_spec(wide, 1), strip],
        [strip] * len(shapes),
        shapes,
        cost(4 * size * size * sz.width // sz.groups, 10 * size * sz.width),
        "middle",
        x,
        wide,
        wide,
        spectrum,
    )


def middle_back_kernel(
    sz, d_ref, third_ref, second_ref, spectrum_ref, mixed_ref, out_ref, grad_ref
):
    d_filtered = mix_rows(sz, third_ref, d_ref[...].astype(F32))
    grad_ref[...] = (d_filtered * mixed_ref[...]).astype(BF16)
    d_mixed = d_filtered * spectrum_ref[...].astype(F32)
    out_ref[...] = mix_rows(sz, second_ref, d_mixed).astype(BF16)


def middle_back(sz, d, wide, spectrum, mixed):
    size = sz.tall * sz.cols
    part = 256
    strip = pl.BlockSpec((size, part), lambda i: (0, i))
    return call(
        functools.partial(middle_back_kernel, sz),
        sz.width // part,
        [strip, wide_spec(wide, 2), wide_spec(wide, 3), strip, strip],
        [strip, strip],
        [jax.ShapeDtypeStruct((size, sz.width), BF16)] * 2,
        cost(4 * size * size * sz.width // sz.groups, 12 * size * sz.width),
        "middle_back",
        d,
        wide,
        wide,
        spectrum,
        mixed,
    )


def tail_front(sz, x_ref, b1_ref, fourth_ref, gain_one, mix_ref):
    x = x_ref[...].astype(F32)
    normed = (x * rms_scale(x) * gain_one).astype(BF16)
    collected = [dot(fourth_ref[r], sz.get(b1_ref, r)) for r in range(sz.per)]
    back = collected[0] if sz.per == 1 else jnp.concatenate(collected, axis=0)
    wide = sz.width // NB
    gate = jnp.concatenate(
        [
            dot(cols_of(normed, b, wide), mix_ref[b * wide : (b + 1) * wide, :])
            for b in range(NB)
        ],
        axis=1,
    )
    y1 = (x + back * gate).astype(BF16)
    return normed, back, gate, y1


def tail_kernel(
    sz,
    x_ref,
    b1_ref,
    fourth_ref,
    gain_one_ref,
    gain_two_ref,
    mix_ref,
    up_ref,
    act_ref,
    down_ref,
    out_ref,
):
    _, _, _, y1 = tail_front(sz, x_ref, b1_ref, fourth_ref, gain_one_ref[...], mix_ref)
    y = y1.astype(F32)
    n2 = (y * rms_scale(y) * gain_two_ref[...]).astype(BF16)
    wide = sz.width // NB
    hidden = []
    for b in range(NB):
        rows = slice(b * wide, (b + 1) * wide)
        lifted = dot(n2[:, rows], up_ref[rows, :])
        gated = dot(n2[:, rows], act_ref[rows, :])
        hidden.append((gated * jax.nn.sigmoid(gated) * lifted).astype(BF16))
    units = hidden[0].shape[1]
    piece = units // NB
    for b in range(NB):
        mixed = jnp.concatenate([cols_of(h, b, piece) for h in hidden], axis=1)
        out_ref[:, b * wide : (b + 1) * wide] = (
            cols_of(y, b, wide) + dot(mixed, down_ref[b * units : (b + 1) * units, :])
        ).astype(BF16)


def tail_specs(sz, weights):
    return [
        sz.token_spec(sz.width),
        sz.sent_spec(),
        sz.factor_spec(),
        whole((1, sz.width)),
        whole((1, sz.width)),
    ] + [whole(w.shape) for w in weights]


def tail_parts(sz, x, b1, fourth, gain_one, gain_two, *weights):
    return (
        functools.partial(tail_kernel, sz),
        sz.rows // sz.per,
        tail_specs(sz, weights),
        [sz.token_spec(sz.width)],
        [jax.ShapeDtypeStruct((sz.tokens, sz.width), BF16)],
        cost(4 * sz.tokens * sz.width * sz.width, 8 * sz.tokens * sz.width),
        "tail",
        x,
        b1,
        fourth,
        gain_one,
        gain_two,
        *weights,
    )


def turn_kernel(
    sz,
    x_ref,
    b1_ref,
    fourth_ref,
    gain_one_ref,
    gain_two_ref,
    mix_ref,
    up_ref,
    act_ref,
    down_ref,
    g_ref,
    sent_ref,
    dy_ref,
    dgate_ref,
    n1_ref,
    n2_ref,
    hs_ref,
    dup_ref,
    dact_ref,
):
    n1, back, gate, y1 = tail_front(sz, x_ref, b1_ref, fourth_ref, gain_one_ref[...], mix_ref)
    n1_ref[...] = n1
    y = y1.astype(F32)
    scale_two = rms_scale(y)
    n2 = (y * scale_two * gain_two_ref[...]).astype(BF16)
    n2_ref[...] = n2
    wide = sz.width // NB
    units = up_ref.shape[1]
    piece = units // NB
    d_shuffled = [
        dot_t(g_ref[:, b * wide : (b + 1) * wide], down_ref[b * units : (b + 1) * units, :]).astype(
            BF16
        )
        for b in range(NB)
    ]
    d_n2 = []
    for b in range(NB):
        rows = slice(b * wide, (b + 1) * wide)
        lifted = dot(n2[:, rows], up_ref[rows, :])
        gated = dot(n2[:, rows], act_ref[rows, :])
        sigma = jax.nn.sigmoid(gated)
        silu = gated * sigma
        hidden = (silu * lifted).astype(BF16)
        for k in range(NB):
            at = k * units + b * piece
            hs_ref[:, at : at + piece] = cols_of(hidden, k, piece)
        d_hidden = jnp.concatenate([cols_of(d, b, piece) for d in d_shuffled], axis=1).astype(F32)
        d_lift = (d_hidden * silu).astype(BF16)
        d_gated = (d_hidden * lifted * sigma * (1.0 + gated * (1.0 - sigma))).astype(BF16)
        dup_ref[:, b * units : (b + 1) * units] = d_lift
        dact_ref[:, b * units : (b + 1) * units] = d_gated
        d_n2.append(dot_t(d_lift, up_ref[rows, :]) + dot_t(d_gated, act_ref[rows, :]))
    d_n2 = jnp.concatenate(d_n2, axis=1)
    dy = (g_ref[...].astype(F32) + norm_back(y, scale_two, gain_two_ref[...], d_n2)).astype(BF16)
    dy_ref[...] = dy
    dyw = dy.astype(F32)
    dgate_ref[...] = (dyw * back).astype(BF16)
    d_back = (dyw * gate).astype(BF16)
    for r in range(sz.per):
        part = d_back[r * sz.line : (r + 1) * sz.line, :]
        sz.put(sent_ref, r, t_dot(fourth_ref[r], part).astype(BF16))


def turn_parts(sz, x, b1, fourth, gain_one, gain_two, mix, up, act, down, g):
    weights = (mix, up, act, down)
    units = NB * up.shape[1]
    widths = [sz.width] * 4 + [units] * 3
    return (
        functools.partial(turn_kernel, sz),
        sz.rows // sz.per,
        tail_specs(sz, weights) + [sz.token_spec(sz.width)],
        [sz.sent_spec()] + [sz.token_spec(w) for w in widths],
        [jax.ShapeDtypeStruct(sz.sent_shape(), BF16)]
        + [jax.ShapeDtypeStruct((sz.tokens, w), BF16) for w in widths],
        cost(8 * sz.tokens * sz.width * sz.width, 30 * sz.tokens * sz.width),
        "turn",
        x,
        b1,
        fourth,
        gain_one,
        gain_two,
        *weights,
        g,
    )


def weights_kernel(factor, share, n1, dgate, n2, dup, dact, hs, g, out_ref):
    wide = n1.shape[1]
    units = dup.shape[1]
    out_ref[:, :wide] = (t_dot(n1[...], dgate[...]) * factor).astype(BF16)
    out_ref[:, wide : wide + units] = (t_dot(n2[...], dup[...]) * factor).astype(BF16)
    out_ref[:, wide + units : wide + 2 * units] = (t_dot(n2[...], dact[...]) * factor).astype(BF16)
    down = (t_dot(hs[...], g[...]) * factor).astype(BF16)
    ratio = units // wide
    for k in range(units // share):
        at = wide + 2 * units + (k % ratio) * wide
        out_ref[(k // ratio) * share : (k // ratio + 1) * share, at : at + wide] = down[
            k * share : (k + 1) * share, :
        ]


def weight_parts(sz, factor, n1, dgate, n2, dup, dact, hs, g):
    wide = sz.width // NB
    units = dup.shape[1] // NB
    total = wide + 3 * units
    slim = pl.BlockSpec((sz.tokens, wide), lambda i: (0, i))
    broad = pl.BlockSpec((sz.tokens, units), lambda i: (0, i))
    return (
        functools.partial(weights_kernel, factor, sz.width // sz.n),
        NB,
        [slim, slim, slim, broad, broad, broad, slim],
        [pl.BlockSpec((wide, total), lambda i: (i, 0))],
        [jax.ShapeDtypeStruct((sz.width, total), BF16)],
        cost(2 * sz.tokens * sz.width * total, 24 * sz.tokens * sz.width),
        "weight_grads",
        n1,
        dgate,
        n2,
        dup,
        dact,
        hs,
        g,
    )


def last_kernel(sz, x_ref, d_ref, first_ref, gain_ref, mix_ref, dgate_ref, dy_ref, out_ref):
    wide = sz.width // NB
    gain = gain_ref[...]
    for r in range(sz.per):
        at = pl.ds(r * sz.line, sz.line)
        gated = jnp.concatenate(
            [
                dot_t(
                    dgate_ref[at, b * wide : (b + 1) * wide], mix_ref[b * wide : (b + 1) * wide, :]
                )
                for b in range(NB)
            ],
            axis=1,
        )
        d_normed = t_dot(first_ref[r], sz.get(d_ref, r)) + gated
        x = x_ref[at, :].astype(F32)
        out_ref[at, :] = (
            dy_ref[at, :].astype(F32) + norm_back(x, rms_scale(x), gain, d_normed)
        ).astype(BF16)


def last(sz, part, x, d, first, gain, mix, dgate, dy):
    steps = sz.rows // sz.per
    skip = part * steps
    tokens = sz.token_spec(sz.width, skip)
    return call(
        functools.partial(last_kernel, sz),
        steps,
        [
            tokens,
            sz.sent_spec(),
            sz.factor_spec(skip),
            whole((1, sz.width)),
            whole(mix.shape),
            tokens,
            tokens,
        ],
        sz.token_spec(sz.width),
        jax.ShapeDtypeStruct((sz.tokens, sz.width), BF16),
        cost(2 * sz.tokens * sz.width * 384, 10 * sz.tokens * sz.width),
        "last",
        x,
        d,
        first,
        gain,
        mix,
        dgate,
        dy,
    )


def join(one, two):
    a, b = len(one[2]), len(two[2])
    c = len(one[3])

    def body(*refs):
        ins, outs = refs[: a + b], refs[a + b :]
        one[0](*ins[:a], *outs[:c])
        two[0](*ins[a:], *outs[c:])

    return (
        (body, one[1], one[2] + two[2], one[3] + two[3], one[4] + two[4], one[5], one[6])
        + tuple(one[7:])
        + tuple(two[7:])
    )


def finish_kernel(
    sz,
    parts,
    send_ref,
    x_ref,
    first_ref,
    gain_ref,
    mix_ref,
    dgate_ref,
    dy_ref,
    out_ref,
    recv,
    dx,
    zero,
    send_sem,
    recv_sem,
    own_sem,
    up_send,
    up_recv,
    zero_sem,
):
    step = pl.program_id(0)
    me, section = lax.axis_index("seq"), lax.axis_index("section")
    sections = lax.axis_size("section")
    some = sz.rows // parts
    wide = sz.width // NB

    def part_exchange(p):
        return exchange(
            sz.n,
            lambda peer: send_ref.at[peer, pl.ds(p * some, some)],
            recv.at[p, me],
            lambda k: send_sem.at[p, k],
            lambda k: recv_sem.at[p, k],
            own_sem.at[p],
        )

    def up_copy(p):
        return pltpu.make_async_remote_copy(
            src_ref=dx.at[p],
            dst_ref=out_ref.at[p],
            send_sem=up_send.at[p],
            recv_sem=up_recv.at[p],
            device_id={"section": lax.rem(section + sections - 1, sections)},
            device_id_type=pl.DeviceIdType.MESH,
        )

    def zero_copy(p):
        return pltpu.make_async_copy(zero, out_ref.at[p], zero_sem.at[p])

    top = section == sections - 1

    @pl.when(step == 0)
    def _():
        greet(
            sz.n,
            [
                {"section": lax.rem(section + 1, sections)},
                {"section": lax.rem(section + sections - 1, sections)},
            ],
        )
        part_exchange(0)[0]()

        @pl.when(top)
        def _():
            zero[...] = jnp.zeros_like(zero)
            for p in range(parts):
                zero_copy(p).start()

    gain = gain_ref[...]
    gated, scales = [], []
    for r in range(some):
        at = pl.ds(r * sz.line, sz.line)
        gated.append(
            jnp.concatenate(
                [
                    dot_t(
                        dgate_ref[at, b * wide : (b + 1) * wide],
                        mix_ref[b * wide : (b + 1) * wide, :],
                    )
                    for b in range(NB)
                ],
                axis=1,
            )
        )
        scales.append(rms_scale(x_ref[at, :].astype(F32)))
    part_exchange(step)[1]()

    @pl.when(step == 0)
    def _():
        for p in range(1, min(parts, 3)):
            part_exchange(p)[0]()

    @pl.when((step > 0) & (step + 2 < parts))
    def _():
        part_exchange(step + 2)[0]()

    for r in range(some):
        at = pl.ds(r * sz.line, sz.line)
        d = recv[step, :, r].reshape(sz.line, sz.width)
        d_normed = t_dot(first_ref[r], d) + gated[r]
        x = x_ref[at, :].astype(F32)
        dx[step, at, :] = (
            dy_ref[at, :].astype(F32) + norm_back(x, scales[r], gain, d_normed)
        ).astype(BF16)

    @pl.when(section > 0)
    def _():
        up_copy(step).start()

    @pl.when(step == parts - 1)
    def _():
        @pl.when(section > 0)
        def _():
            for p in range(parts):
                up_copy(p).wait_send()

        @pl.when(section < sections - 1)
        def _():
            for p in range(parts):
                up_copy(p).wait_recv()

        @pl.when(top)
        def _():
            for p in range(parts):
                zero_copy(p).wait()


def finish(sz, parts, cid, d, x, first, gain, mix, dgate, dy):
    some = sz.rows // parts
    tokens = some * sz.line
    strip = pl.BlockSpec((tokens, sz.width), lambda i: (i, 0))
    out = pl.pallas_call(
        functools.partial(finish_kernel, sz, parts),
        grid=(parts,),
        in_specs=[
            pl.BlockSpec(memory_space=pl.ANY),
            strip,
            pl.BlockSpec((some, sz.line, sz.line), lambda i: (i, 0, 0)),
            whole((1, sz.width)),
            whole(mix.shape),
            strip,
            strip,
        ],
        out_specs=pl.BlockSpec(memory_space=pl.ANY),
        out_shape=jax.ShapeDtypeStruct((parts, tokens, sz.width), BF16),
        scratch_shapes=[
            pltpu.VMEM((parts, sz.n, some, sz.cols, sz.width), BF16),
            pltpu.VMEM((parts, tokens, sz.width), BF16),
            pltpu.VMEM((tokens, sz.width), BF16),
            pltpu.SemaphoreType.DMA((parts, sz.n - 1)),
            pltpu.SemaphoreType.DMA((parts, sz.n - 1)),
            pltpu.SemaphoreType.DMA((parts,)),
            pltpu.SemaphoreType.DMA((parts,)),
            pltpu.SemaphoreType.DMA((parts,)),
            pltpu.SemaphoreType.DMA((parts,)),
        ],
        compiler_params=pltpu.CompilerParams(
            dimension_semantics=("arbitrary",),
            vmem_limit_bytes=VMEM,
            collective_id=cid,
            has_side_effects=True,
        ),
        cost_estimate=cost(2 * sz.tokens * sz.width * 384, 10 * sz.tokens * sz.width),
        name="finish",
    )(d, x, first, gain, mix, dgate, dy)
    return out.reshape(sz.tokens, sz.width)


def split_kernel(wide, units, total, mix_ref, up_ref, act_ref, down_ref):
    mix_ref[...] = total[:, :wide]
    up_ref[...] = total[:, wide : wide + units]
    act_ref[...] = total[:, wide + units : wide + 2 * units]
    share = total.shape[0]
    for k in range(units // wide):
        at = wide + 2 * units + k * wide
        down_ref[k * share : (k + 1) * share, :] = total[:, at : at + wide]


def split_grads(total, wide, units):
    share = total.shape[0]
    shapes = [(share, wide), (share, units), (share, units), (share * units // wide, wide)]
    return call(
        functools.partial(split_kernel, wide, units),
        1,
        [whole(total.shape)],
        [whole(shape) for shape in shapes],
        [jax.ShapeDtypeStruct(shape, BF16) for shape in shapes],
        cost(0, 4 * share * (wide + 3 * units)),
        "split_grads",
        total,
    )


def shift(array, by):
    length = lax.axis_size("section")
    pairs = [(i, i + by) for i in range(length) if 0 <= i + by < length]
    return lax.ppermute(array, "section", pairs)


def shards(
    section_input,
    stashed_input,
    output_grad,
    gain_mixer,
    gain_channel,
    factor_first,
    factor_second,
    spectrum,
    factor_third,
    factor_fourth,
    mixer_gate,
    channel_up,
    channel_gate,
    channel_down,
):
    first = factor_first[0]
    fourth = factor_fourth[0]
    n = lax.axis_size("seq")
    rows = first.shape[0]
    cols = factor_second.shape[1]
    width = section_input.shape[2]
    sz = Sizes(n, rows, cols, width)
    size = sz.tall * cols
    kernel_here = spectrum[0].reshape(size, width)
    mix, up, act, down = mixer_gate[0], channel_up[0], channel_gate[0], channel_down[0]
    gain_one, gain_two = gain_mixer, gain_channel
    xa, xb, g = section_input[0], stashed_input[0], output_grad[0]
    factor = 1.0 / math.sqrt(sz.tall * sz.line)

    everything = (0, rows)
    weights = (mix, up, act, down)
    (sent_b,) = call(*front_parts(sz, xb, gain_one, first))
    recv_b, sent_a, wide = call_exchanging(
        sz,
        sz.to_send(sent_b),
        everything,
        1,
        *front_expand_parts(sz, xa, gain_one, first, factor_second[0], factor_third[0]),
    )
    recv_a, out_b, mixed_b = call_exchanging(
        sz,
        sz.to_send(sent_a),
        everything,
        2,
        *middle_parts(sz, sz.to_flat(recv_b), wide, kernel_here, True),
    )
    rows_b, out_a = call_exchanging(
        sz,
        sz.from_flat(out_b),
        everything,
        3,
        *middle_parts(sz, sz.to_flat(recv_a), wide, kernel_here, False),
    )
    rows_a, sent, dy, dgate, n1, n2, hs, dup, dact = call_exchanging(
        sz,
        sz.from_flat(out_a),
        everything,
        4,
        *turn_parts(sz, xb, sz.to_rows(rows_b), fourth, gain_one, gain_two, *weights, g),
    )
    work = tail_parts(sz, xa, sz.to_rows(rows_a), fourth, gain_one, gain_two, *weights)
    more = weight_parts(sz, factor, n1, dgate, n2, dup, dact, hs, g)
    if work[1] == more[1]:
        d_cols, out, grads = call_exchanging(
            sz, sz.to_send(sent), everything, 5, *join(work, more)
        )
    else:
        d_cols, out = call_exchanging(sz, sz.to_send(sent), everything, 5, *work)
        (grads,) = call(*more)
    next_input = shift(out, 1)
    d_out, spectrum_grad = middle_back(sz, sz.to_flat(d_cols), wide, kernel_here, mixed_b)
    d_out = sz.from_flat(d_out)
    parts = max(k for k in (1, 2, 4, 8) if rows % k == 0)
    some = rows // parts
    sp = Sizes(n, some, cols, width)
    grads, d_out = lax.optimization_barrier((grads, d_out))
    total = lax.psum_scatter(grads, "seq", scatter_dimension=0, tiled=True)
    if sz.aligned:
        upstream = finish(sz, parts, 6, d_out, xb, first, gain_one, mix, dgate, dy)
    else:
        dx = []
        for part in range(parts):
            work = (lambda: None, 1, [], [], [], cost(0, 0), "rest")
            (d_rows,) = call_exchanging(sz, d_out, (part * some, some), 6 + part, *work)
            dx.append(last(sp, part, xb, sp.to_rows(d_rows), first, gain_one, mix, dgate, dy))
        upstream = shift(jnp.concatenate(dx, axis=0), -1)
    grads = split_grads(total, width // NB, up.shape[1])
    return (
        next_input[None],
        upstream[None],
        spectrum_grad.reshape(spectrum.shape),
    ) + tuple(grad[None] for grad in grads)


def solution(mesh):
    in_specs = (
        P("section", "seq", None),
        P("section", "seq", None),
        P("section", "seq", None),
        P("section", None),
        P("section", None),
        P("section", "seq", None, None),
        P("section", "seq", None, None),
        P("section", None, "seq", None),
        P("section", "seq", None, None),
        P("section", "seq", None, None),
        P("section", None, None),
        P("section", None, None),
        P("section", None, None),
        P("section", None, None),
    )
    out_specs = (
        P("section", "seq", None),
        P("section", "seq", None),
        P("section", None, "seq", None),
        P("section", "seq", None),
        P("section", "seq", None),
        P("section", "seq", None),
        P("section", "seq", None),
    )
    return jax.shard_map(shards, mesh=mesh, in_specs=in_specs, out_specs=out_specs, check_vma=False)
```
